32 devices in a mesh: hrow: 4 (over z), hcol: 8 (over y, x, core).
Axes of the slice: x: 2, y: 2, z: 4, core: 2. Of those that a mesh axis runs over, the one named last changes fastest.
Arguments:
- expect: bfloat16 [2, 256, 25600], P(None, 'hrow', 'hcol'), may hold values from -6 to 6
- distrib: bfloat16 [2, 256, 25600], P(None, 'hrow', 'hcol'), may hold values from -0.0048828125 to 0.0048828125
- direct: float32 [2, 2, 256], P(None, None, 'hcol'), may hold values from -4 to 4
- pair_index: int32 [4, 2], replicated, may hold values from 0 to 1
Outputs:
- jacobian: float32 [4, 256, 256], P(None, 'hrow', 'hcol')
The draws below stay inside these ranges and needn't reach their ends.
Inputs may be any that keep to these rules, and one draw needn't show every extreme that they name: `pair_index`: column 0 of each row names a shock and column 1 an output; pairs may repeat.
All inputs are finite; a program needn't handle non-finite values.
Results may differ from the reference program's by a relative error of at most 0.0003.
Values may be sent and summed in bfloat16 or wider, within the bound.
No kernel may reach another device: no remote copies, remote signals or barrier semaphores. Data moves between devices by JAX's collectives and lax.ppermute only.
A program may use at most 64 MiB of HBM per device.

```python
import jax
import jax.numpy as jnp
from jax import lax

SHOCKS = 2
OUTPUTS = 2
PAIRS = 4
HORIZON = 256
GRID = 25600


def set_ends(values, key, smallest, largest):
    spot = [jax.random.randint(jax.random.fold_in(key, axis), (), 0, length) for axis, length in enumerate(values.shape)]
    main_axis = values.shape.index(max(values.shape))
    beside = spot[:main_axis] + [(spot[main_axis] + 1) % values.shape[main_axis]] + spot[main_axis + 1:]
    return values.at[tuple(spot)].set(smallest).at[tuple(beside)].set(largest)


def steps_of(own_key, extent, cuts, least, top_value):
    def one(position, blocks):
        draws = jax.random.uniform(jax.random.fold_in(jax.random.fold_in(own_key, 6), position), (blocks,), jnp.float32, least / len(cuts), top_value / len(cuts))
        return jnp.repeat(jnp.exp(draws), extent[position] // blocks).reshape((-1,) + (1,) * (len(extent) - position - 1))

    loudness = one(*cuts[0])
    for cut in cuts[1:]:
        loudness = loudness * one(*cut)
    return loudness


def noise(rng, dims, spread, bound, split=(), dtype=jnp.bfloat16):
    entries = spread * jax.random.normal(rng, dims, jnp.float32)
    if split:
        entries = entries * steps_of(rng, dims, split, -0.22, 0.18)
    return jnp.clip(entries, -bound, bound).astype(dtype)


def setup_inputs(seed: int = 0) -> dict:
    keys = jax.random.split(jax.random.key(seed), 5)
    expect = noise(keys[0], (OUTPUTS, HORIZON, GRID), 1.0, 6.0, ((1, 4), (2, 8)))
    distrib = noise(keys[1], (SHOCKS, HORIZON, GRID), (64 * GRID) ** -0.5, 0.0048828125, ((1, 4), (2, 8)))
    direct = noise(keys[2], (SHOCKS, OUTPUTS, HORIZON), 0.5, 4.0, ((2, 8),), jnp.float32)
    pair_index = set_ends(jax.random.randint(keys[3], (PAIRS, 2), 0, SHOCKS), jax.random.fold_in(keys[3], 1), 0, SHOCKS - 1).astype(jnp.int32)
    return dict(expect=expect, distrib=distrib, direct=direct, pair_index=pair_index)


def reference(expect, distrib, direct, pair_index):
    results = []
    for which in range(PAIRS):
        shock_id = pair_index[which, 0]
        output_id = pair_index[which, 1]
        outcome = jnp.take(expect, output_id, axis=0)
        response = jnp.take(distrib, shock_id, axis=0)
        fake_news = jnp.dot(outcome, response.T, preferred_element_type=jnp.float32)
        first_row = jnp.take(jnp.take(direct, shock_id, axis=0), output_id, axis=0)
        fake_news = fake_news.at[0].add(first_row)

        def advance(previous, current):
            moved_prev = jnp.concatenate([jnp.zeros((1,), jnp.float32), previous[:-1]])
            summed = current + moved_prev
            return summed, summed

        _, jacob_pair = lax.scan(advance, jnp.zeros((HORIZON,), jnp.float32), fake_news)
        results.append(jacob_pair)
    return jnp.stack(results)
```

```python
import functools

import jax
import jax.numpy as jnp
from jax import lax
from jax.experimental import pallas as pl
from jax.experimental.pallas import tpu as pltpu
from jax.sharding import PartitionSpec as P

LANES = 128
VMEM_BYTES = 56 * 1024 * 1024


def swap(block, axis, mask):
    return lax.ppermute(block, axis, [(i, i ^ mask) for i in range(lax.axis_size(axis))])


def gather_rows_kernel(width, spot_ref, own_ref, *refs):
    *received, out_ref = refs
    rows = own_ref.shape[1]
    z = spot_ref[0]
    out_ref[:, :, width:] = jnp.zeros(out_ref.shape[:2] + (out_ref.shape[2] - width,), out_ref.dtype)
    out_ref[:, pl.ds(pl.multiple_of(z * rows, rows), rows), :] = own_ref[...]
    for mask, ref in enumerate(received, 1):
        out_ref[:, pl.ds(pl.multiple_of((z ^ mask) * rows, rows), rows), :width] = ref[...]


def partial_kernel(shock, spot_ref, expect_ref, direct_ref, *refs):
    *pieces, keep_ref, give_ref, responses, products = refs
    rows = pieces[0].shape[0]
    half = rows // 2
    horizon = products.shape[0]
    z = spot_ref[0]
    core = spot_ref[1]
    for mask, ref in enumerate(pieces):
        responses[pl.ds(pl.multiple_of((z ^ mask) * rows, rows), rows), :] = ref[...]
    step = 256
    row_id = lax.broadcasted_iota(jnp.int32, (rows, horizon), 0)
    date_id = lax.broadcasted_iota(jnp.int32, (rows, horizon), 1)
    for output in range(expect_ref.shape[0]):
        for start in range(0, horizon, step):
            products[start : start + step, :] = lax.dot_general(
                responses[start : start + step, :],
                expect_ref[output],
                (((1,), (1,)), ((), ())),
                preferred_element_type=jnp.float32,
            )

        def one_block(index, carry):
            block = products[pl.ds(pl.multiple_of(index * rows, rows), rows), :]
            added = direct_ref[shock, output, pl.ds(pl.multiple_of(index * rows, rows), rows), :]
            block = block + jnp.where(date_id == 0, added, 0.0)
            offset = 1
            while offset < rows:
                moved = pltpu.roll(pltpu.roll(block, offset, 1), offset, 0)
                inside = (row_id >= offset) & (date_id >= offset)
                block = block + jnp.where(inside, moved, 0.0)
                offset = offset * 2
            spread = jnp.broadcast_to(carry, (rows, horizon))
            moved = pltpu.roll(spread, 1, 1, stride=1, stride_axis=0)
            block = block + jnp.where(date_id > row_id, moved, 0.0)
            low = block[:half]
            high = block[half:]
            keep_ref[index, output] = jnp.where(core == 0, low, high)
            give_ref[index, output] = jnp.where(core == 0, high, low)
            return block[rows - 1 :]

        lax.fori_loop(0, horizon // rows, one_block, jnp.zeros((1, horizon), jnp.float32))


def pack_kernel(spot_ref, *refs):
    planes = (len(refs) - 1) // 2
    parts = refs[: len(refs) - 1 - planes]
    outs = refs[len(parts) : -1]
    cut = refs[-1]
    z = spot_ref[0]
    total = parts[0][...]
    for ref in parts[1:]:
        total = total + ref[...]
    width = total.shape[2] // len(outs)
    for plane in range(len(outs)):
        piece = total[:, :, plane * width : (plane + 1) * width]
        cut[plane] = jnp.concatenate([piece[o] for o in range(piece.shape[0])], axis=1)
    for mask, ref in enumerate(outs):
        ref[...] = cut[z ^ mask]


def finish_kernel(planes, pair_ref, *refs):
    *parts, out_ref, picked = refs
    rows = out_ref.shape[1]
    for shock in range(len(parts) // planes):
        total = parts[shock * planes][...]
        for ref in parts[shock * planes + 1 : (shock + 1) * planes]:
            total = total + ref[...]
        turned = total.T
        for output in range(turned.shape[0] // rows):
            picked[shock, output] = turned[output * rows : (output + 1) * rows]
    for pair in range(out_ref.shape[0]):
        out_ref[pair] = picked[pair_ref[pair, 0], pair_ref[pair, 1]]


def call(kernel, name, out_shape, scalars, arrays, scratch=()):
    specs = [pl.BlockSpec(memory_space=pltpu.SMEM)]
    specs += [pl.BlockSpec(memory_space=pltpu.VMEM)] * len(arrays)
    return pl.pallas_call(
        kernel,
        name=name,
        out_shape=out_shape,
        in_specs=specs,
        out_specs=jax.tree.map(lambda _: pl.BlockSpec(memory_space=pltpu.VMEM), out_shape),
        scratch_shapes=list(scratch),
        compiler_params=pltpu.CompilerParams(vmem_limit_bytes=VMEM_BYTES),
    )(scalars, *arrays)


def shards(expect, distrib, direct, pair_index):
    planes = lax.axis_size("hrow")
    col_devices = lax.axis_size("hcol")
    chips = col_devices // 2
    outputs, rows, grid = expect.shape
    shocks = distrib.shape[0]
    horizon = rows * planes
    cols = horizon // col_devices
    pairs = pair_index.shape[0]
    z = lax.axis_index("hrow")
    c = lax.axis_index("hcol")
    chip = c // 2
    spot = jnp.stack([z, c % 2]).astype(jnp.int32)

    width = grid // LANES // planes * LANES
    rest = grid - width * planes

    def cut(values, plane):
        return lax.dynamic_slice_in_dim(values, plane * width, width, axis=-1)

    def with_rest(values, plane):
        return jnp.concatenate([cut(values, plane), values[..., grid - rest :]], axis=-1)

    masks = range(1, planes)
    expect_in = [swap(cut(expect, z ^ m), "hrow", m) for m in masks]
    expect_all = call(
        functools.partial(gather_rows_kernel, width),
        "gather_rows",
        jax.ShapeDtypeStruct((outputs, horizon, width + rest), expect.dtype),
        spot,
        [with_rest(expect, z)] + expect_in,
    )

    top = jnp.where(z == 0, direct, jnp.zeros_like(direct))
    top = lax.dynamic_update_slice_in_dim(
        jnp.zeros((shocks, outputs, horizon), jnp.float32), top, c * cols, axis=2
    )[..., None]

    done = []
    for shock in range(shocks):
        own = with_rest(distrib[shock], z)
        received = [swap(with_rest(distrib[shock], z ^ m), "hrow", m) for m in masks]
        part = jax.ShapeDtypeStruct((chips, outputs, cols, horizon), jnp.float32)
        keep, give = call(
            functools.partial(partial_kernel, shock),
            f"partial_{shock}",
            (part, part),
            spot,
            [expect_all, top, own] + received,
            [
                pltpu.VMEM((horizon, width + rest), distrib.dtype),
                pltpu.VMEM((horizon, horizon), jnp.float32),
            ],
        )
        chip_sums = keep + swap(give, "hcol", 1)

        def of_chip(index):
            return lax.dynamic_index_in_dim(chip_sums, index, 0, False)

        parts = [of_chip(chip)] + [swap(of_chip(chip ^ m), "hcol", 2 * m) for m in range(1, chips)]
        packed = jax.ShapeDtypeStruct((cols, outputs * rows), jnp.float32)
        pieces = call(
            pack_kernel,
            f"pack_{shock}",
            (packed,) * planes,
            spot,
            parts,
            [pltpu.VMEM((planes, cols, outputs * rows), jnp.float32)],
        )
        done += [pieces[0]] + [swap(pieces[m], "hrow", m) for m in masks]

    return call(
        functools.partial(finish_kernel, planes),
        "finish",
        jax.ShapeDtypeStruct((pairs, rows, cols), jnp.float32),
        pair_index,
        done,
        [pltpu.VMEM((shocks, outputs, rows, cols), jnp.float32)],
    )


def solution(mesh):
    placed = (P(None, "hrow", "hcol"), P(None, "hrow", "hcol"), P(None, None, "hcol"), P())
    return jax.shard_map(
        shards, mesh=mesh, in_specs=placed, out_specs=P(None, "hrow", "hcol"), check_vma=False
    )
```

```python
import functools
import math

import jax
import jax.numpy as jnp
from jax import lax
from jax.experimental import pallas as pl
from jax.experimental.pallas import tpu as pltpu
from jax.sharding import PartitionSpec as P

LANES = 128


def swap(block, axis, mask):
    return lax.ppermute(block, axis, [(i, i ^ mask) for i in range(lax.axis_size(axis))])


def add_diagonals(block):
    rows, dates = block.shape
    row_id = lax.broadcasted_iota(jnp.int32, (rows, dates), 0)
    date_id = lax.broadcasted_iota(jnp.int32, (rows, dates), 1)
    least = jnp.minimum(row_id, date_id)
    offset = 1
    while offset < rows:
        moved = pltpu.roll(pltpu.roll(block, offset, 1), offset, 0)
        block = block + jnp.where(least >= offset, moved, 0.0)
        offset = offset * 2
    return block, row_id, date_id


def partial_sums(shock, spot_ref, expect_at, direct_ref, keep_ref, give_ref, responses, products):
    horizon = products.shape[0]
    half = keep_ref.shape[2]
    step = min(horizon, 256)
    z = spot_ref[0]
    core = spot_ref[1]
    mine = pl.ds(pl.multiple_of(spot_ref[2] * half, half), half)
    first = lax.broadcasted_iota(jnp.int32, (half, LANES), 1) == 0
    for output in range(keep_ref.shape[1]):
        for start in range(0, horizon, step):
            products[start : start + step, :] = lax.dot_general(
                responses[start : start + step, :],
                expect_at(output),
                (((1,), (1,)), ((), ())),
                preferred_element_type=jnp.float32,
            )
        column = shock * keep_ref.shape[1] + output
        added = jnp.where(first & (z == 0), direct_ref[:, column : column + 1], 0.0)
        products[mine, :LANES] = products[mine, :LANES] + added
        last = None
        for start in range(0, horizon, step):
            block, row_id, date_id = add_diagonals(products[start : start + step, :])
            if last is not None:
                spread = jnp.broadcast_to(last, block.shape)
                moved = pltpu.roll(spread, 1, 1, stride=1, stride_axis=0)
                block = block + jnp.where(date_id > row_id, moved, 0.0)
            last = block[step - 1 :]
            for pair in range(step // (2 * half)):
                low = block[2 * pair * half : (2 * pair + 1) * half]
                high = block[(2 * pair + 1) * half : (2 * pair + 2) * half]
                keep_ref[start // (2 * half) + pair, output] = jnp.where(core == 0, low, high)
                give_ref[start // (2 * half) + pair, output] = jnp.where(core == 0, high, low)


def place(z, mask, rows):
    return pl.ds(pl.multiple_of((z ^ mask) * rows, rows), rows)


def first_kernel(width, planes, spot_ref, direct_ref, *refs):
    pieces = refs[:planes]
    expect_ref, keep_ref, give_ref, responses, products = refs[planes:]
    outputs = expect_ref.shape[0]
    rows = pieces[0].shape[0]
    z = spot_ref[0]
    expect_ref[:, :, width:] = jnp.zeros_like(expect_ref[:, :, width:])
    for mask, ref in enumerate(pieces):
        for output in range(outputs):
            expect_ref[output, place(z, mask, rows), :width] = ref[
                :, output * width : (output + 1) * width
            ]
        responses[place(z, mask, rows), :] = ref[:, outputs * width : outputs * width + responses.shape[1]]
    rest = responses.shape[1] - width
    for output in range(outputs):
        begin = outputs * width + responses.shape[1] + output * rest
        expect_ref[output, place(z, 0, rows), width:] = pieces[0][:, begin : begin + rest]
    partial_sums(
        0, spot_ref, lambda o: expect_ref[o], direct_ref, keep_ref, give_ref, responses, products
    )


def next_kernel(shock, planes, spot_ref, direct_ref, expect_ref, *refs):
    pieces = refs[:planes]
    keep_ref, give_ref, responses, products = refs[planes:]
    rows = pieces[0].shape[0]
    z = spot_ref[0]
    for mask, ref in enumerate(pieces):
        responses[place(z, mask, rows), :] = ref[...]
    partial_sums(
        shock, spot_ref, lambda o: expect_ref[o], direct_ref, keep_ref, give_ref, responses, products
    )


def pack_kernel(chips, planes, spot_ref, *refs):
    parts, outs, cut = refs[: len(refs) - 1 - planes], refs[-1 - planes : -1], refs[-1]
    z = spot_ref[0]
    for shock in range(len(parts) // chips):
        total = parts[shock * chips][...]
        for ref in parts[shock * chips + 1 : (shock + 1) * chips]:
            total = total + ref[...]
        width = total.shape[2] // planes
        for plane in range(planes):
            piece = total[:, :, plane * width : (plane + 1) * width]
            cut[plane, shock] = jnp.concatenate([piece[o] for o in range(piece.shape[0])], axis=1)
    for mask, ref in enumerate(outs):
        ref[...] = cut[z ^ mask]


def finish_kernel(pair_ref, *refs):
    *parts, out_ref, picked = refs
    rows = out_ref.shape[2]
    total = parts[0][...]
    for ref in parts[1:]:
        total = total + ref[...]
    for output in range(picked.shape[1]):
        picked[:, output] = total[:, :, output * rows : (output + 1) * rows]
    for pair in range(out_ref.shape[0]):
        out_ref[pair] = picked[pair_ref[pair, 0], pair_ref[pair, 1]]


def size_of(leaf):
    shape = leaf.shape[:-1] + (-(-leaf.shape[-1] // LANES) * LANES,)
    return math.prod(shape) * leaf.dtype.itemsize


def call(kernel, name, out_shape, scalars, arrays, scratch):
    held = sum(size_of(leaf) for leaf in jax.tree.leaves((arrays, out_shape)))
    held += sum(size_of(leaf) for leaf in scratch)
    return pl.pallas_call(
        kernel,
        name=name,
        out_shape=out_shape,
        in_specs=[pl.BlockSpec(memory_space=pltpu.SMEM)]
        + [pl.BlockSpec(memory_space=pltpu.VMEM)] * len(arrays),
        out_specs=jax.tree.map(lambda _: pl.BlockSpec(memory_space=pltpu.VMEM), out_shape),
        scratch_shapes=scratch,
        compiler_params=pltpu.CompilerParams(vmem_limit_bytes=held * 3 // 2 + (4 << 20)),
    )(scalars, *arrays)


def shards(expect, distrib, direct, pair_index):
    planes = lax.axis_size("hrow")
    col_devices = lax.axis_size("hcol")
    chips = col_devices // 2
    outputs, rows, grid = expect.shape
    shocks = distrib.shape[0]
    horizon = rows * planes
    cols = horizon // col_devices
    pairs = pair_index.shape[0]
    z = lax.axis_index("hrow")
    c = lax.axis_index("hcol")
    chip = c // 2
    spot = jnp.stack([z, c % 2, c]).astype(jnp.int32)

    width = grid // LANES // planes * LANES
    rest = grid - width * planes

    def cut(values, plane):
        return lax.dynamic_slice_in_dim(values, plane * width, width, axis=-1)

    def responses(shock, plane):
        return [cut(distrib[shock], plane), distrib[shock, :, grid - rest :]]

    def first_message(plane):
        return [cut(expect[o], plane) for o in range(outputs)] + responses(0, plane)

    masks = range(1, planes)
    own = jnp.concatenate(first_message(z) + [expect[o, :, grid - rest :] for o in range(outputs)], axis=1)
    pieces = [own] + [
        swap(jnp.concatenate(first_message(z ^ m), axis=1), "hrow", m) for m in masks
    ]
    later = [
        [jnp.concatenate(responses(shock, z), axis=1)]
        + [swap(jnp.concatenate(responses(shock, z ^ m), axis=1), "hrow", m) for m in masks]
        for shock in range(1, shocks)
    ]
    flat = direct.reshape(shocks * outputs, cols).T

    part = jax.ShapeDtypeStruct((chips, outputs, cols, horizon), jnp.float32)
    scratch = [
        pltpu.VMEM((horizon, width + rest), distrib.dtype),
        pltpu.VMEM((horizon, horizon), jnp.float32),
    ]
    parts = []
    for shock in range(shocks):
        if shock == 0:
            expect_all, keep, give = call(
                functools.partial(first_kernel, width, planes),
                "partial_0",
                (jax.ShapeDtypeStruct((outputs, horizon, width + rest), expect.dtype), part, part),
                spot,
                [flat] + pieces,
                scratch,
            )
        else:
            keep, give = call(
                functools.partial(next_kernel, shock, planes),
                f"partial_{shock}",
                (part, part),
                spot,
                [flat, expect_all] + later[shock - 1],
                scratch,
            )
        chip_sums = keep + swap(give, "hcol", 1)

        def of_chip(index):
            return lax.dynamic_index_in_dim(chip_sums, index, 0, False)

        parts += [of_chip(chip)] + [swap(of_chip(chip ^ m), "hcol", 2 * m) for m in range(1, chips)]

    packed = jax.ShapeDtypeStruct((shocks, cols, outputs * rows), jnp.float32)
    cuts = call(
        functools.partial(pack_kernel, chips, planes),
        "pack",
        (packed,) * planes,
        spot,
        parts,
        [pltpu.VMEM((planes, shocks, cols, outputs * rows), jnp.float32)],
    )
    turned = call(
        finish_kernel,
        "finish",
        jax.ShapeDtypeStruct((pairs, cols, rows), jnp.float32),
        pair_index,
        [cuts[0]] + [swap(cuts[m], "hrow", m) for m in masks],
        [pltpu.VMEM((shocks, outputs, cols, rows), jnp.float32)],
    )
    return jnp.swapaxes(turned, 1, 2)


def solution(mesh):
    placed = (P(None, "hrow", "hcol"), P(None, "hrow", "hcol"), P(None, None, "hcol"), P())
    return jax.shard_map(
        shards, mesh=mesh, in_specs=placed, out_specs=P(None, "hrow", "hcol"), check_vma=False
    )
```

```python
import functools
import math

import jax
import jax.numpy as jnp
from jax import lax
from jax.experimental import pallas as pl
from jax.experimental.pallas import tpu as pltpu
from jax.sharding import PartitionSpec as P

LANES = 128
FIRST = 1


def swap(block, axis, mask):
    return lax.ppermute(block, axis, [(i, i ^ mask) for i in range(lax.axis_size(axis))])


def add_diagonals(block):
    rows, dates = block.shape
    row_id = lax.broadcasted_iota(jnp.int32, (rows, dates), 0)
    date_id = lax.broadcasted_iota(jnp.int32, (rows, dates), 1)
    least = jnp.minimum(row_id, date_id)
    offset = 1
    while offset < rows:
        moved = pltpu.roll(pltpu.roll(block, offset, 1), offset, 0)
        block = block + jnp.where(least >= offset, moved, 0.0)
        offset = offset * 2
    return block, row_id, date_id


def cut_kernel(width, planes, masks, rests, counts, *refs):
    arrays = refs[: len(rests)]
    *messages, sems = refs[len(rests) :]
    grid = arrays[0].shape[1]
    rest = grid - width * planes
    z = lax.axis_index("hrow")
    copies = []

    def copy(source, begin, size, goal, column):
        part = source.at[:, pl.ds(begin, size)]
        copies.append(pltpu.make_async_copy(part, goal.at[:, pl.ds(column, size)], sems.at[len(copies)]))
        copies[-1].start()

    for message, mask, count in zip(messages, masks, counts):
        begin = pl.multiple_of((z ^ mask) * width, LANES)
        column = 0
        for source, with_rest in zip(arrays[:count], rests):
            copy(source, begin, width, message, column)
            column = column + width
            if with_rest or mask == 0:
                copy(source, grid - rest, rest, message, column)
                column = column + rest
    for one in copies:
        one.wait()


def partial_sums(shocks, expect_ref, direct_ref, keep_ref, give_ref, responses, products):
    outputs, horizon = products.shape[:2]
    chips, planes, _, half, lanes = keep_ref.shape
    width = lanes // outputs
    step = min(horizon, 256)
    z = lax.axis_index("hrow")
    c = lax.axis_index("hcol")
    core = c % 2
    mine = pl.ds(pl.multiple_of(c * half, half), half)
    first = lax.broadcasted_iota(jnp.int32, (half, LANES), 1) == 0
    for index, shock in enumerate(shocks):
        for output in range(outputs):
            for start in range(0, horizon, step):
                products[output, start : start + step, :] = lax.dot_general(
                    responses[index, start : start + step, :],
                    expect_ref[output],
                    (((1,), (1,)), ((), ())),
                    preferred_element_type=jnp.float32,
                )
            added = jnp.where(first & (z == 0), direct_ref[shock * outputs + output], 0.0)
            products[output, mine, :LANES] = products[output, mine, :LANES] + added
        last = [None] * outputs
        for start in range(0, horizon, step):
            blocks = []
            for output in range(outputs):
                block, row_id, date_id = add_diagonals(products[output, start : start + step, :])
                if last[output] is not None:
                    spread = jnp.broadcast_to(last[output], block.shape)
                    moved = pltpu.roll(spread, 1, 1, stride=1, stride_axis=0)
                    block = block + jnp.where(date_id > row_id, moved, 0.0)
                last[output] = block[step - 1 :]
                blocks.append(block)
            for plane in range(planes):
                dates = slice(plane * width, (plane + 1) * width)
                both = jnp.concatenate([block[:, dates] for block in blocks], axis=1)
                for part in range(step // (2 * half)):
                    low = both[2 * part * half : (2 * part + 1) * half]
                    high = both[(2 * part + 1) * half : (2 * part + 2) * half]
                    chip = start // (2 * half) + part
                    keep_ref[chip, plane, index] = jnp.where(core == 0, low, high)
                    give_ref[chip, plane, index] = jnp.where(core == 0, high, low)


def place(z, mask, rows):
    return pl.ds(pl.multiple_of((z ^ mask) * rows, rows), rows)


def first_kernel(width, planes, shocks, direct_ref, *refs):
    messages = refs[:planes]
    expect_ref, keep_ref, give_ref, responses, products = refs[planes:]
    outputs, _, depth = expect_ref.shape
    rows = messages[0].shape[0]
    z = lax.axis_index("hrow")
    expect_ref[:, :, width:] = jnp.zeros_like(expect_ref[:, :, width:])
    for mask, ref in enumerate(messages):
        size = width if mask else depth
        for o in range(outputs):
            expect_ref[o, place(z, mask, rows), :size] = ref[:, o * size : (o + 1) * size]
        for index in range(len(shocks)):
            begin = outputs * size + index * depth
            responses[index, place(z, mask, rows), :] = ref[:, begin : begin + depth]
    partial_sums(shocks, expect_ref, direct_ref, keep_ref, give_ref, responses, products)


def next_kernel(begins, shocks, direct_ref, expect_ref, *refs):
    messages = refs[: len(begins)]
    keep_ref, give_ref, responses, products = refs[len(begins) :]
    rows, depth = messages[0].shape[0], responses.shape[2]
    z = lax.axis_index("hrow")
    for mask, (ref, begin) in enumerate(zip(messages, begins)):
        for index in range(len(shocks)):
            column = begin + index * depth
            responses[index, place(z, mask, rows), :] = ref[:, column : column + depth]
    partial_sums(shocks, expect_ref, direct_ref, keep_ref, give_ref, responses, products)


def size_of(leaf):
    shape = leaf.shape[:-1] + (-(-leaf.shape[-1] // LANES) * LANES,)
    return math.prod(shape) * leaf.dtype.itemsize


def call(kernel, name, out_shape, arrays, scratch=(), scalars=(), flops=0, source=pltpu.VMEM):
    held = sum(size_of(leaf) for leaf in jax.tree.leaves((arrays, out_shape)))
    taken = held + sum(size_of(leaf) for leaf in scratch if isinstance(leaf, jax.ShapeDtypeStruct) or jnp.issubdtype(leaf.dtype, jnp.number))
    return pl.pallas_call(
        kernel,
        name=name,
        out_shape=out_shape,
        in_specs=[pl.BlockSpec(memory_space=pltpu.SMEM)] * len(scalars)
        + [pl.BlockSpec(memory_space=source)] * len(arrays),
        out_specs=jax.tree.map(lambda _: pl.BlockSpec(memory_space=pltpu.VMEM), out_shape),
        scratch_shapes=scratch,
        cost_estimate=pl.CostEstimate(flops=flops, bytes_accessed=held, transcendentals=0),
        compiler_params=pltpu.CompilerParams(vmem_limit_bytes=taken * 3 // 2 + (4 << 20)),
    )(*scalars, *arrays)


def shards(expect, distrib, direct, pair_index):
    planes = lax.axis_size("hrow")
    col_devices = lax.axis_size("hcol")
    chips = col_devices // 2
    outputs, rows, grid = expect.shape
    shocks = distrib.shape[0]
    horizon = rows * planes
    cols = horizon // col_devices
    pairs = pair_index.shape[0]
    width = grid // LANES // planes * LANES
    rest = grid - width * planes
    depth = width + rest
    masks = range(1, planes)

    def cut(name, arrays, rests, sent, counts):
        shapes = [
            jax.ShapeDtypeStruct(
                (rows, sum(depth if with_rest or m == 0 else width for with_rest in rests[:count])),
                expect.dtype,
            )
            for m, count in zip(sent, counts)
        ]
        return call(
            functools.partial(cut_kernel, width, planes, sent, rests, counts),
            name,
            shapes,
            arrays,
            [pltpu.SemaphoreType.DMA((2 * sum(counts),))],
            source=pl.ANY,
        )

    def to_planes(messages, sent):
        return [swap(message, "hrow", m) if m else message for m, message in zip(sent, messages)]

    z = lax.axis_index("hrow")
    chip = lax.axis_index("hcol") // 2
    flat = direct.reshape(shocks * outputs, cols, 1)

    def kernel_call(kernel, name, group, arrays, extra=()):
        part = jax.ShapeDtypeStruct((chips, planes, len(group), cols, outputs * rows), jnp.float32)
        return call(
            kernel,
            name,
            (*extra, part, part),
            arrays,
            [
                pltpu.VMEM((len(group), horizon, depth), distrib.dtype),
                pltpu.VMEM((outputs, horizon, horizon), jnp.float32),
            ],
            flops=2 * len(group) * outputs * horizon * horizon * depth,
        )

    def scattered(values, own, axis, masks, scale, joined):
        def block(index):
            return jnp.concatenate(
                [lax.dynamic_index_in_dim(value, index, 0, False) for value in values], axis=joined
            )

        return functools.reduce(
            jnp.add, [block(own)] + [swap(block(own ^ m), axis, scale * m) for m in masks]
        )

    def over_cores(keep, give):
        return keep + swap(give, "hcol", 1)

    group = range(FIRST)
    rest_group = range(FIRST, shocks)
    arrays = [expect[o] for o in range(outputs)] + [distrib[s] for s in range(shocks)]
    rests = (False,) * outputs + (True,) * shocks
    some = outputs + len(group)
    counts = [len(arrays) if m < 2 else some for m in range(planes)]
    first = to_planes(cut("cut_0", arrays, rests, range(planes), counts), range(planes))
    if rest_group:
        later = cut("cut_1", arrays[some:], rests[some:], range(2, planes), [len(rest_group)] * (planes - 2))
        later = first[:2] + to_planes(later, range(2, planes))
    whole = jax.ShapeDtypeStruct((outputs, horizon, depth), expect.dtype)
    expect_all, *parts = kernel_call(
        functools.partial(first_kernel, width, planes, group), "partial_0", group, [flat] + first, [whole]
    )
    sums = [over_cores(*parts)]
    if rest_group:
        begins = [some * depth, outputs * width + len(group) * depth] + [0] * (planes - 2)
        parts = kernel_call(
            functools.partial(next_kernel, begins, rest_group),
            "partial_1",
            rest_group,
            [flat, expect_all] + later,
        )
        sums.append(over_cores(*parts))

    chip_sum = scattered(sums, chip, "hcol", range(1, chips), 2, 1)
    total = scattered([chip_sum], z, "hrow", range(1, planes), 1, 0)
    shock_of = pair_index[:, 0, None, None]
    output_of = pair_index[:, 1, None, None]
    picked = jnp.zeros((pairs, cols, rows), jnp.float32)
    for s in range(shocks):
        for o in range(outputs):
            one = total[s, :, o * rows : (o + 1) * rows]
            picked = jnp.where((shock_of == s) & (output_of == o), one, picked)
    return jnp.swapaxes(picked, 1, 2)


def solution(mesh):
    placed = (P(None, "hrow", "hcol"), P(None, "hrow", "hcol"), P(None, None, "hcol"), P())
    return jax.shard_map(
        shards, mesh=mesh, in_specs=placed, out_specs=P(None, "hrow", "hcol"), check_vma=False
    )
```

```python
import functools
import math

import jax
import jax.numpy as jnp
from jax import lax
from jax.experimental import pallas as pl
from jax.experimental.pallas import tpu as pltpu
from jax.sharding import PartitionSpec as P

LANES = 128
FIRST = 1


def swap(block, axis, mask):
    return lax.ppermute(block, axis, [(i, i ^ mask) for i in range(lax.axis_size(axis))])


def add_diagonals(block):
    rows, dates = block.shape
    row_id = lax.broadcasted_iota(jnp.int32, (rows, dates), 0)
    date_id = lax.broadcasted_iota(jnp.int32, (rows, dates), 1)
    least = jnp.minimum(row_id, date_id)
    offset = 1
    while offset < rows:
        moved = pltpu.roll(pltpu.roll(block, offset, 1), offset, 0)
        block = block + jnp.where(least >= offset, moved, 0.0)
        offset = offset * 2
    return block, row_id, date_id


def packed_share(planes, arrays, rest):
    share = rest // planes
    return share if rest == LANES and share * arrays <= LANES and share * planes == rest else 0


def cut_kernel(width, planes, masks, counts, tail_at, *refs):
    arrays = list(refs[: len(refs) - len(masks) - 1])
    *messages, sems = refs[len(arrays) :]
    rows, grid = arrays[0].shape
    rest = grid - width * planes
    share = packed_share(planes, len(arrays), rest)
    z = lax.axis_index("hrow")
    copies = []

    def copy(source, begin, size, goal, column):
        part = source.at[:, pl.ds(begin, size)]
        copies.append(pltpu.make_async_copy(part, goal.at[:, pl.ds(column, size)], sems.at[len(copies)]))
        copies[-1].start()

    for message, mask, count in zip(messages, masks, counts):
        begin = pl.multiple_of((z ^ mask) * width, LANES)
        for index, source in enumerate(arrays[:count]):
            copy(source, begin, width, message, index * width)
        if tail_at is not None and not share:
            last = arrays[tail_at:] + (arrays[:tail_at] if mask == 0 else [])
            for index, source in enumerate(last):
                copy(source, grid - rest, rest, message, count * width + index * rest)
    if tail_at is not None and share:
        spot = lax.broadcasted_iota(jnp.int32, (rows, LANES), 1)
        tails = [source[:, grid - rest :].astype(jnp.float32) for source in arrays]
        for message, mask, count in zip(messages, masks, counts):
            tile = jnp.zeros((rows, LANES), jnp.float32)
            for index, tail in enumerate(tails):
                shift = lax.rem(index * share + LANES - (z ^ mask) * share, LANES)
                inside = (spot >= index * share) & (spot < (index + 1) * share)
                tile = jnp.where(inside, pltpu.roll(tail, shift, 1), tile)
            message[:, count * width : count * width + LANES] = tile.astype(message.dtype)
    for one in copies:
        one.wait()


def partial_sums(shocks, expect_ref, direct_ref, keep_ref, give_ref, responses, products):
    outputs, horizon = products.shape[:2]
    chips, planes, _, half, lanes = keep_ref.shape
    width = lanes // outputs
    step = min(horizon, 256)
    z = lax.axis_index("hrow")
    c = lax.axis_index("hcol")
    core = c % 2
    mine = pl.ds(pl.multiple_of(c * half, half), half)
    first = lax.broadcasted_iota(jnp.int32, (half, LANES), 1) == 0
    for index, shock in enumerate(shocks):
        for output in range(outputs):
            for start in range(0, horizon, step):
                products[output, start : start + step, :] = lax.dot_general(
                    responses[index, start : start + step, :],
                    expect_ref[output],
                    (((1,), (1,)), ((), ())),
                    preferred_element_type=jnp.float32,
                )
            added = jnp.where(first & (z == 0), direct_ref[shock * outputs + output], 0.0)
            products[output, mine, :LANES] = products[output, mine, :LANES] + added
        last = [None] * outputs
        for start in range(0, horizon, step):
            blocks = []
            for output in range(outputs):
                block, row_id, date_id = add_diagonals(products[output, start : start + step, :])
                if last[output] is not None:
                    spread = jnp.broadcast_to(last[output], block.shape)
                    moved = pltpu.roll(spread, 1, 1, stride=1, stride_axis=0)
                    block = block + jnp.where(date_id > row_id, moved, 0.0)
                last[output] = block[step - 1 :]
                blocks.append(block)
            for plane in range(planes):
                dates = slice(plane * width, (plane + 1) * width)
                both = jnp.concatenate([block[:, dates] for block in blocks], axis=1)
                for part in range(step // (2 * half)):
                    low = both[2 * part * half : (2 * part + 1) * half]
                    high = both[(2 * part + 1) * half : (2 * part + 2) * half]
                    chip = start // (2 * half) + part
                    keep_ref[chip, plane, index] = jnp.where(core == 0, low, high)
                    give_ref[chip, plane, index] = jnp.where(core == 0, high, low)


def place(z, mask, rows):
    return pl.ds(pl.multiple_of((z ^ mask) * rows, rows), rows)


def first_kernel(width, planes, counts, shocks, direct_ref, *refs):
    messages = refs[:planes]
    expect_ref, tails_ref, keep_ref, give_ref, responses, products = refs[planes:]
    outputs = expect_ref.shape[0]
    rows = messages[0].shape[0]
    rest = tails_ref.shape[2]
    arrays = outputs + tails_ref.shape[0]
    share = packed_share(planes, arrays, rest)
    z = lax.axis_index("hrow")
    inside = lax.broadcasted_iota(jnp.int32, (rows, rest), 1) < share
    if not share:
        expect_ref[:, :, width:] = jnp.zeros_like(expect_ref[:, :, width:])
    for mask, (ref, count) in enumerate(zip(messages, counts)):
        spot = place(z, mask, rows)
        for o in range(outputs):
            expect_ref[o, spot, :width] = ref[:, o * width : (o + 1) * width]
        for index in range(len(shocks)):
            responses[index, spot, :width] = ref[:, (outputs + index) * width : (outputs + index + 1) * width]
        tail = count * width
        if share:
            tile = ref[:, tail : tail + rest].astype(jnp.float32)
            for index in range(arrays):
                moved = tile if index == 0 else pltpu.roll(tile, LANES - index * share, 1)
                moved = jnp.where(inside, moved, 0.0).astype(ref.dtype)
                if index < outputs:
                    expect_ref[index, spot, width:] = moved
                else:
                    tails_ref[index - outputs, spot, :] = moved
        else:
            for index in range(arrays if mask == 0 else arrays - outputs):
                moved = ref[:, tail + index * rest : tail + (index + 1) * rest]
                if index < arrays - outputs:
                    tails_ref[index, spot, :] = moved
                else:
                    expect_ref[index - arrays + outputs, spot, width:] = moved
    for index, shock in enumerate(shocks):
        responses[index, :, width:] = tails_ref[shock]
    partial_sums(shocks, expect_ref, direct_ref, keep_ref, give_ref, responses, products)


def next_kernel(width, begins, shocks, direct_ref, expect_ref, tails_ref, *refs):
    messages = refs[: len(begins)]
    keep_ref, give_ref, responses, products = refs[len(begins) :]
    rows = messages[0].shape[0]
    z = lax.axis_index("hrow")
    for index, shock in enumerate(shocks):
        for mask, (ref, begin) in enumerate(zip(messages, begins)):
            column = begin + index * width
            responses[index, place(z, mask, rows), :width] = ref[:, column : column + width]
        responses[index, :, width:] = tails_ref[shock]
    partial_sums(shocks, expect_ref, direct_ref, keep_ref, give_ref, responses, products)


def size_of(leaf):
    shape = leaf.shape[:-1] + (-(-leaf.shape[-1] // LANES) * LANES,)
    return math.prod(shape) * leaf.dtype.itemsize


def call(kernel, name, out_shape, arrays, scratch=(), scalars=(), flops=0):
    held = sum(size_of(leaf) for leaf in jax.tree.leaves((arrays, out_shape)))
    taken = held + sum(size_of(leaf) for leaf in scratch if isinstance(leaf, jax.ShapeDtypeStruct) or jnp.issubdtype(leaf.dtype, jnp.number))
    return pl.pallas_call(
        kernel,
        name=name,
        out_shape=out_shape,
        in_specs=[pl.BlockSpec(memory_space=pltpu.SMEM)] * len(scalars)
        + [pl.BlockSpec(memory_space=pltpu.VMEM)] * len(arrays),
        out_specs=jax.tree.map(lambda _: pl.BlockSpec(memory_space=pltpu.VMEM), out_shape),
        scratch_shapes=scratch,
        cost_estimate=pl.CostEstimate(flops=flops, bytes_accessed=held, transcendentals=0),
        compiler_params=pltpu.CompilerParams(vmem_limit_bytes=taken * 3 // 2 + (4 << 20)),
    )(*scalars, *arrays)


def shards(expect, distrib, direct, pair_index):
    planes = lax.axis_size("hrow")
    col_devices = lax.axis_size("hcol")
    chips = col_devices // 2
    outputs, rows, grid = expect.shape
    shocks = distrib.shape[0]
    horizon = rows * planes
    cols = horizon // col_devices
    pairs = pair_index.shape[0]
    width = grid // LANES // planes * LANES
    rest = grid - width * planes
    depth = width + rest
    share = packed_share(planes, outputs + shocks, rest)

    def cut(name, arrays, sent, counts, tail_at=None):
        def columns(m, count):
            if tail_at is None or share:
                return count * width + (0 if tail_at is None else LANES)
            return count * width + (len(arrays) if m == 0 else len(arrays) - tail_at) * rest

        return call(
            functools.partial(cut_kernel, width, planes, sent, counts, tail_at),
            name,
            [jax.ShapeDtypeStruct((rows, columns(m, count)), expect.dtype) for m, count in zip(sent, counts)],
            arrays,
            [pltpu.SemaphoreType.DMA((sum(counts) + len(sent) * len(arrays),))],
        )

    def to_planes(messages, sent):
        return [swap(message, "hrow", m) if m else message for m, message in zip(sent, messages)]

    z = lax.axis_index("hrow")
    chip = lax.axis_index("hcol") // 2
    flat = direct.reshape(shocks * outputs, cols, 1)

    def kernel_call(kernel, name, group, arrays, extra=()):
        part = jax.ShapeDtypeStruct((chips, planes, len(group), cols, outputs * rows), jnp.float32)
        return call(
            kernel,
            name,
            (*extra, part, part),
            arrays,
            [
                pltpu.VMEM((len(group), horizon, depth), distrib.dtype),
                pltpu.VMEM((outputs, horizon, horizon), jnp.float32),
            ],
            flops=2 * len(group) * outputs * horizon * horizon * depth,
        )

    def scattered(values, own, axis, masks, scale, joined):
        def block(index):
            return jnp.concatenate(
                [lax.dynamic_index_in_dim(value, index, 0, False) for value in values], axis=joined
            )

        return functools.reduce(
            jnp.add, [block(own)] + [swap(block(own ^ m), axis, scale * m) for m in masks]
        )

    def over_cores(keep, give):
        return keep + swap(give, "hcol", 1)

    group = range(FIRST)
    rest_group = range(FIRST, shocks)
    arrays = [expect[o] for o in range(outputs)] + [distrib[s] for s in range(shocks)]
    some = outputs + len(group)
    counts = [len(arrays) if m < 2 else some for m in range(planes)]
    first = to_planes(cut("cut_0", arrays, range(planes), counts, outputs), range(planes))
    if rest_group:
        later = cut("cut_1", arrays[some:], range(2, planes), [len(rest_group)] * (planes - 2))
        later = first[:2] + to_planes(later, range(2, planes))
    expect_all, tails, *parts = kernel_call(
        functools.partial(first_kernel, width, planes, counts, group),
        "partial_0",
        group,
        [flat] + first,
        [
            jax.ShapeDtypeStruct((outputs, horizon, depth), expect.dtype),
            jax.ShapeDtypeStruct((shocks, horizon, rest), distrib.dtype),
        ],
    )
    sums = [over_cores(*parts)]
    if rest_group:
        begins = [some * width] * 2 + [0] * (planes - 2)
        parts = kernel_call(
            functools.partial(next_kernel, width, begins, rest_group),
            "partial_1",
            rest_group,
            [flat, expect_all, tails] + later,
        )
        sums.append(over_cores(*parts))

    chip_sum = scattered(sums, chip, "hcol", range(chips - 1, 0, -1), 2, 1)
    total = scattered([chip_sum], z, "hrow", [planes - 1, *range(1, planes - 1)], 1, 0)
    shock_of = pair_index[:, 0, None, None]
    output_of = pair_index[:, 1, None, None]
    picked = jnp.zeros((pairs, cols, rows), jnp.float32)
    for s in range(shocks):
        for o in range(outputs):
            one = total[s, :, o * rows : (o + 1) * rows]
            picked = jnp.where((shock_of == s) & (output_of == o), one, picked)
    return jnp.swapaxes(picked, 1, 2)


def solution(mesh):
    placed = (P(None, "hrow", "hcol"), P(None, "hrow", "hcol"), P(None, None, "hcol"), P())
    return jax.shard_map(
        shards, mesh=mesh, in_specs=placed, out_specs=P(None, "hrow", "hcol"), check_vma=False
    )
```

```python
import functools
import math

import jax
import jax.numpy as jnp
from jax import lax
from jax.experimental import pallas as pl
from jax.experimental.pallas import tpu as pltpu
from jax.sharding import PartitionSpec as P

LANES = 128
FIRST = 1


def swap(block, axis, mask):
    return lax.ppermute(block, axis, [(i, i ^ mask) for i in range(lax.axis_size(axis))])


def add_diagonals(block):
    rows, dates = block.shape
    row_id = lax.broadcasted_iota(jnp.int32, (rows, dates), 0)
    date_id = lax.broadcasted_iota(jnp.int32, (rows, dates), 1)
    least = jnp.minimum(row_id, date_id)
    offset = 1
    while offset < rows:
        moved = pltpu.roll(pltpu.roll(block, offset, 1), offset, 0)
        block = block + jnp.where(least >= offset, moved, 0.0)
        offset = offset * 2
    return block, row_id, date_id


def packed_share(planes, arrays, rest):
    share = rest // planes
    return share if rest == LANES and share * arrays <= LANES and share * planes == rest else 0


def cut_kernel(width, planes, masks, counts, tail_at, *refs):
    arrays = list(refs[: len(refs) - len(masks) - 1])
    *messages, sems = refs[len(arrays) :]
    rows, grid = arrays[0].shape
    rest = grid - width * planes
    share = packed_share(planes, len(arrays), rest)
    z = lax.axis_index("hrow")
    copies = []

    def copy(source, begin, size, goal, column):
        part = source.at[:, pl.ds(begin, size)]
        copies.append(pltpu.make_async_copy(part, goal.at[:, pl.ds(column, size)], sems.at[len(copies)]))
        copies[-1].start()

    for message, mask, count in zip(messages, masks, counts):
        begin = pl.multiple_of((z ^ mask) * width, LANES)
        for index, source in enumerate(arrays[:count]):
            copy(source, begin, width, message, index * width)
        if tail_at is not None and not share:
            last = arrays[tail_at:] + (arrays[:tail_at] if mask == 0 else [])
            for index, source in enumerate(last):
                copy(source, grid - rest, rest, message, count * width + index * rest)
    if tail_at is not None and share:
        spot = lax.broadcasted_iota(jnp.int32, (rows, LANES), 1)
        tails = [source[:, grid - rest :].astype(jnp.float32) for source in arrays]
        for message, mask, count in zip(messages, masks, counts):
            tile = jnp.zeros((rows, LANES), jnp.float32)
            for index, tail in enumerate(tails):
                shift = lax.rem(index * share + LANES - (z ^ mask) * share, LANES)
                inside = (spot >= index * share) & (spot < (index + 1) * share)
                tile = jnp.where(inside, pltpu.roll(tail, shift, 1), tile)
            message[:, count * width : count * width + LANES] = tile.astype(message.dtype)
    for one in copies:
        one.wait()


def partial_sums(shocks, expect_ref, direct_ref, keep_ref, give_ref, responses, products):
    outputs, horizon = products.shape[:2]
    chips, planes, _, half, lanes = keep_ref.shape
    width = lanes // outputs
    step = min(horizon, 256)
    z = lax.axis_index("hrow")
    c = lax.axis_index("hcol")
    core = c % 2
    mine = pl.ds(pl.multiple_of(c * half, half), half)
    first = lax.broadcasted_iota(jnp.int32, (half, LANES), 1) == 0
    for index, shock in enumerate(shocks):
        for output in range(outputs):
            for start in range(0, horizon, step):
                products[output, start : start + step, :] = lax.dot_general(
                    responses[index, start : start + step, :],
                    expect_ref[output],
                    (((1,), (1,)), ((), ())),
                    preferred_element_type=jnp.float32,
                )
            added = jnp.where(first & (z == 0), direct_ref[shock * outputs + output], 0.0)
            products[output, mine, :LANES] = products[output, mine, :LANES] + added
        last = [None] * outputs
        for start in range(0, horizon, step):
            blocks = []
            for output in range(outputs):
                block, row_id, date_id = add_diagonals(products[output, start : start + step, :])
                if last[output] is not None:
                    spread = jnp.broadcast_to(last[output], block.shape)
                    moved = pltpu.roll(spread, 1, 1, stride=1, stride_axis=0)
                    block = block + jnp.where(date_id > row_id, moved, 0.0)
                last[output] = block[step - 1 :]
                blocks.append(block)
            for plane in range(planes):
                dates = slice(plane * width, (plane + 1) * width)
                both = jnp.concatenate([block[:, dates] for block in blocks], axis=1)
                for part in range(step // (2 * half)):
                    low = both[2 * part * half : (2 * part + 1) * half]
                    high = both[(2 * part + 1) * half : (2 * part + 2) * half]
                    chip = start // (2 * half) + part
                    keep_ref[chip, plane, index] = jnp.where(core == 0, low, high)
                    give_ref[chip, plane, index] = jnp.where(core == 0, high, low)


def place(z, mask, rows):
    return pl.ds(pl.multiple_of((z ^ mask) * rows, rows), rows)


def first_kernel(width, planes, counts, shocks, direct_ref, *refs):
    messages = refs[:planes][::-1]
    expect_ref, tails_ref, keep_ref, give_ref, responses, products = refs[planes:]
    outputs = expect_ref.shape[0]
    rows = messages[0].shape[0]
    rest = tails_ref.shape[2]
    arrays = outputs + tails_ref.shape[0]
    share = packed_share(planes, arrays, rest)
    z = lax.axis_index("hrow")
    inside = lax.broadcasted_iota(jnp.int32, (rows, rest), 1) < share
    if not share:
        expect_ref[:, :, width:] = jnp.zeros_like(expect_ref[:, :, width:])
    for mask, (ref, count) in enumerate(zip(messages, counts)):
        spot = place(z, mask, rows)
        for o in range(outputs):
            expect_ref[o, spot, :width] = ref[:, o * width : (o + 1) * width]
        for index in range(len(shocks)):
            responses[index, spot, :width] = ref[:, (outputs + index) * width : (outputs + index + 1) * width]
        tail = count * width
        if share:
            tile = ref[:, tail : tail + rest].astype(jnp.float32)
            for index in range(arrays):
                moved = tile if index == 0 else pltpu.roll(tile, LANES - index * share, 1)
                moved = jnp.where(inside, moved, 0.0).astype(ref.dtype)
                if index < outputs:
                    expect_ref[index, spot, width:] = moved
                else:
                    tails_ref[index - outputs, spot, :] = moved
        else:
            for index in range(arrays if mask == 0 else arrays - outputs):
                moved = ref[:, tail + index * rest : tail + (index + 1) * rest]
                if index < arrays - outputs:
                    tails_ref[index, spot, :] = moved
                else:
                    expect_ref[index - arrays + outputs, spot, width:] = moved
    for index, shock in enumerate(shocks):
        responses[index, :, width:] = tails_ref[shock]
    partial_sums(shocks, expect_ref, direct_ref, keep_ref, give_ref, responses, products)


def next_kernel(width, begins, shocks, direct_ref, expect_ref, tails_ref, *refs):
    messages = refs[: len(begins)]
    keep_ref, give_ref, responses, products = refs[len(begins) :]
    rows = messages[0].shape[0]
    z = lax.axis_index("hrow")
    for index, shock in enumerate(shocks):
        for mask, (ref, begin) in enumerate(zip(messages, begins)):
            column = begin + index * width
            responses[index, place(z, mask, rows), :width] = ref[:, column : column + width]
        responses[index, :, width:] = tails_ref[shock]
    partial_sums(shocks, expect_ref, direct_ref, keep_ref, give_ref, responses, products)


def size_of(leaf):
    shape = leaf.shape[:-1] + (-(-leaf.shape[-1] // LANES) * LANES,)
    return math.prod(shape) * leaf.dtype.itemsize


def call(kernel, name, out_shape, arrays, scratch=(), scalars=(), flops=0):
    held = sum(size_of(leaf) for leaf in jax.tree.leaves((arrays, out_shape)))
    taken = held + sum(size_of(leaf) for leaf in scratch if isinstance(leaf, jax.ShapeDtypeStruct) or jnp.issubdtype(leaf.dtype, jnp.number))
    return pl.pallas_call(
        kernel,
        name=name,
        out_shape=out_shape,
        in_specs=[pl.BlockSpec(memory_space=pltpu.SMEM)] * len(scalars)
        + [pl.BlockSpec(memory_space=pltpu.VMEM)] * len(arrays),
        out_specs=jax.tree.map(lambda _: pl.BlockSpec(memory_space=pltpu.VMEM), out_shape),
        scratch_shapes=scratch,
        cost_estimate=pl.CostEstimate(flops=flops, bytes_accessed=held, transcendentals=0),
        compiler_params=pltpu.CompilerParams(vmem_limit_bytes=taken * 3 // 2 + (4 << 20)),
    )(*scalars, *arrays)


def shards(expect, distrib, direct, pair_index):
    planes = lax.axis_size("hrow")
    col_devices = lax.axis_size("hcol")
    chips = col_devices // 2
    outputs, rows, grid = expect.shape
    shocks = distrib.shape[0]
    horizon = rows * planes
    cols = horizon // col_devices
    pairs = pair_index.shape[0]
    width = grid // LANES // planes * LANES
    rest = grid - width * planes
    depth = width + rest
    share = packed_share(planes, outputs + shocks, rest)
    masks = range(1, planes)

    def cut(name, arrays, sent, counts, tail_at=None):
        def columns(m, count):
            if tail_at is None or share:
                return count * width + (0 if tail_at is None else LANES)
            return count * width + (len(arrays) if m == 0 else len(arrays) - tail_at) * rest

        return call(
            functools.partial(cut_kernel, width, planes, sent, counts, tail_at),
            name,
            [jax.ShapeDtypeStruct((rows, columns(m, count)), expect.dtype) for m, count in zip(sent, counts)],
            arrays,
            [pltpu.SemaphoreType.DMA((sum(counts) + len(sent) * len(arrays),))],
        )

    def to_planes(messages, sent):
        return [swap(message, "hrow", m) if m else message for m, message in zip(sent, messages)]

    z = lax.axis_index("hrow")
    chip = lax.axis_index("hcol") // 2
    flat = direct.reshape(shocks * outputs, cols, 1)

    def kernel_call(kernel, name, group, arrays, extra=()):
        part = jax.ShapeDtypeStruct((chips, planes, len(group), cols, outputs * rows), jnp.float32)
        return call(
            kernel,
            name,
            (*extra, part, part),
            arrays,
            [
                pltpu.VMEM((len(group), horizon, depth), distrib.dtype),
                pltpu.VMEM((outputs, horizon, horizon), jnp.float32),
            ],
            flops=2 * len(group) * outputs * horizon * horizon * depth,
        )

    def scattered(values, own, axis, masks, scale, joined):
        def block(index):
            return jnp.concatenate(
                [lax.dynamic_index_in_dim(value, index, 0, False) for value in values], axis=joined
            )

        return functools.reduce(
            jnp.add, [block(own)] + [swap(block(own ^ m), axis, scale * m) for m in masks]
        )

    def over_cores(keep, give):
        return keep + swap(give, "hcol", 1)

    group = range(FIRST)
    rest_group = range(FIRST, shocks)
    arrays = [expect[o] for o in range(outputs)] + [distrib[s] for s in range(shocks)]
    some = outputs + len(group)
    counts = [len(arrays)] + [some] * (planes - 1)
    first = to_planes(cut("cut_0", arrays, range(planes), counts, outputs), range(planes))
    if rest_group:
        later = cut("cut_1", arrays[some:], masks, [len(rest_group)] * len(masks))
        later = first[:1] + to_planes(later, masks)
    expect_all, tails, *parts = kernel_call(
        functools.partial(first_kernel, width, planes, counts, group),
        "partial_0",
        group,
        [flat] + first[::-1],
        [
            jax.ShapeDtypeStruct((outputs, horizon, depth), expect.dtype),
            jax.ShapeDtypeStruct((shocks, horizon, rest), distrib.dtype),
        ],
    )
    sums = [over_cores(*parts)]
    if rest_group:
        begins = [some * width] + [0] * len(masks)
        parts = kernel_call(
            functools.partial(next_kernel, width, begins, rest_group),
            "partial_1",
            rest_group,
            [flat, expect_all, tails] + later,
        )
        sums.append(over_cores(*parts))

    chip_sum = scattered(sums, chip, "hcol", range(chips - 1, 0, -1), 2, 1)
    total = scattered([chip_sum], z, "hrow", [planes - 1, *range(1, planes - 1)], 1, 0)
    shock_of = pair_index[:, 0, None, None]
    output_of = pair_index[:, 1, None, None]
    picked = jnp.zeros((pairs, cols, rows), jnp.float32)
    for s in range(shocks):
        for o in range(outputs):
            one = total[s, :, o * rows : (o + 1) * rows]
            picked = jnp.where((shock_of == s) & (output_of == o), one, picked)
    return jnp.swapaxes(picked, 1, 2)


def solution(mesh):
    placed = (P(None, "hrow", "hcol"), P(None, "hrow", "hcol"), P(None, None, "hcol"), P())
    return jax.shard_map(
        shards, mesh=mesh, in_specs=placed, out_specs=P(None, "hrow", "hcol"), check_vma=False
    )
```

```python
import functools
import math

import jax
import jax.numpy as jnp
from jax import lax
from jax.experimental import pallas as pl
from jax.experimental.pallas import tpu as pltpu
from jax.sharding import PartitionSpec as P

LANES = 128
FIRST = 1


def swap(block, axis, mask):
    return lax.ppermute(block, axis, [(i, i ^ mask) for i in range(lax.axis_size(axis))])


def add_diagonals(block):
    rows, dates = block.shape
    lane = lax.broadcasted_iota(jnp.int32, (rows, LANES), 1)
    top_row = lax.broadcasted_iota(jnp.int32, (8, LANES), 0)
    tiles = [block[:, start : start + LANES] for start in range(0, dates, LANES)]
    offset = 1
    while offset < rows:
        moved = tiles
        if offset % LANES:
            turned = [pltpu.roll(tile, offset % LANES, 1) for tile in tiles]
            behind = [jnp.zeros_like(turned[0])] + turned[:-1]
            moved = [jnp.where(lane < offset % LANES, low, high) for low, high in zip(behind, turned)]
        past = offset // LANES
        sums = tiles[:past]
        for tile, more in zip(tiles[past:], moved[: len(tiles) - past]):
            if offset % 8:
                more = pltpu.roll(more, offset, 0)
                more = jnp.concatenate([jnp.where(top_row < offset, 0.0, more[:8]), more[8:]], axis=0)
                sums.append(tile + more)
            else:
                sums.append(jnp.concatenate([tile[:offset], tile[offset:] + more[: rows - offset]], axis=0))
        tiles = sums
        offset = offset * 2
    return jnp.concatenate(tiles, axis=1)


def packed_share(planes, arrays, rest):
    share = rest // planes
    return share if rest == LANES and share * arrays <= LANES and share * planes == rest else 0


def cut_kernel(width, planes, masks, counts, tail_at, *refs):
    arrays = list(refs[: len(refs) - len(masks) - 1])
    *messages, sems = refs[len(arrays) :]
    rows, grid = arrays[0].shape
    rest = grid - width * planes
    share = packed_share(planes, len(arrays), rest)
    z = lax.axis_index("hrow")
    copies = []

    def copy(source, begin, size, goal, column):
        part = source.at[:, pl.ds(begin, size)]
        copies.append(pltpu.make_async_copy(part, goal.at[:, pl.ds(column, size)], sems.at[len(copies)]))
        copies[-1].start()

    for message, mask, count in zip(messages, masks, counts):
        begin = pl.multiple_of((z ^ mask) * width, LANES)
        for index, source in enumerate(arrays[:count]):
            copy(source, begin, width, message, index * width)
        if tail_at is not None and not share:
            last = arrays[tail_at:] + (arrays[:tail_at] if mask == 0 else [])
            for index, source in enumerate(last):
                copy(source, grid - rest, rest, message, count * width + index * rest)
    if tail_at is not None and share:
        spot = lax.broadcasted_iota(jnp.int32, (rows, LANES), 1)
        tails = [source[:, grid - rest :].astype(jnp.float32) for source in arrays]
        for message, mask, count in zip(messages, masks, counts):
            tile = jnp.zeros((rows, LANES), jnp.float32)
            for index, tail in enumerate(tails):
                shift = lax.rem(index * share + LANES - (z ^ mask) * share, LANES)
                inside = (spot >= index * share) & (spot < (index + 1) * share)
                tile = jnp.where(inside, pltpu.roll(tail, shift, 1), tile)
            message[:, count * width : count * width + LANES] = tile.astype(message.dtype)
    for one in copies:
        one.wait()


def partial_sums(shocks, expect_ref, direct_ref, keep_ref, give_ref, responses, products):
    outputs, horizon = products.shape[:2]
    chips, planes, _, half, lanes = keep_ref.shape
    width = lanes // outputs
    step = min(horizon, 256)
    z = lax.axis_index("hrow")
    c = lax.axis_index("hcol")
    core = c % 2
    mine = pl.ds(pl.multiple_of(c * half, half), half)
    first = lax.broadcasted_iota(jnp.int32, (half, LANES), 1) == 0
    for index, shock in enumerate(shocks):
        for output in range(outputs):
            for start in range(0, horizon, step):
                products[output, start : start + step, :] = lax.dot_general(
                    responses[index, start : start + step, :],
                    expect_ref[output],
                    (((1,), (1,)), ((), ())),
                    preferred_element_type=jnp.float32,
                )
            added = jnp.where(first & (z == 0), direct_ref[shock * outputs + output], 0.0)
            products[output, mine, :LANES] = products[output, mine, :LANES] + added
        last = [None] * outputs
        for start in range(0, horizon, step):
            blocks = []
            for output in range(outputs):
                block = add_diagonals(products[output, start : start + step, :])
                if last[output] is not None:
                    spread = jnp.broadcast_to(last[output], block.shape)
                    moved = pltpu.roll(spread, 1, 1, stride=1, stride_axis=0)
                    row_id = lax.broadcasted_iota(jnp.int32, block.shape, 0)
                    date_id = lax.broadcasted_iota(jnp.int32, block.shape, 1)
                    block = block + jnp.where(date_id > row_id, moved, 0.0)
                last[output] = block[step - 1 :]
                blocks.append(block)
            for plane in range(planes):
                dates = slice(plane * width, (plane + 1) * width)
                both = jnp.concatenate([block[:, dates] for block in blocks], axis=1)
                for part in range(step // (2 * half)):
                    low = both[2 * part * half : (2 * part + 1) * half]
                    high = both[(2 * part + 1) * half : (2 * part + 2) * half]
                    chip = start // (2 * half) + part
                    keep_ref[chip, plane, index] = jnp.where(core == 0, low, high)
                    give_ref[chip, plane, index] = jnp.where(core == 0, high, low)


def place(z, mask, rows):
    return pl.ds(pl.multiple_of((z ^ mask) * rows, rows), rows)


def first_kernel(width, planes, counts, shocks, direct_ref, *refs):
    messages = refs[:planes][::-1]
    expect_ref, tails_ref, keep_ref, give_ref, responses, products = refs[planes:]
    outputs = expect_ref.shape[0]
    rows = messages[0].shape[0]
    rest = tails_ref.shape[2]
    arrays = outputs + tails_ref.shape[0]
    share = packed_share(planes, arrays, rest)
    z = lax.axis_index("hrow")
    inside = lax.broadcasted_iota(jnp.int32, (rows, rest), 1) < share
    if not share:
        expect_ref[:, :, width:] = jnp.zeros_like(expect_ref[:, :, width:])
    for mask, (ref, count) in enumerate(zip(messages, counts)):
        spot = place(z, mask, rows)
        for o in range(outputs):
            expect_ref[o, spot, :width] = ref[:, o * width : (o + 1) * width]
        for index in range(len(shocks)):
            responses[index, spot, :width] = ref[:, (outputs + index) * width : (outputs + index + 1) * width]
        tail = count * width
        if share:
            tile = ref[:, tail : tail + rest].astype(jnp.float32)
            for index in range(arrays):
                moved = tile if index == 0 else pltpu.roll(tile, LANES - index * share, 1)
                moved = jnp.where(inside, moved, 0.0).astype(ref.dtype)
                if index < outputs:
                    expect_ref[index, spot, width:] = moved
                else:
                    tails_ref[index - outputs, spot, :] = moved
        else:
            for index in range(arrays if mask == 0 else arrays - outputs):
                moved = ref[:, tail + index * rest : tail + (index + 1) * rest]
                if index < arrays - outputs:
                    tails_ref[index, spot, :] = moved
                else:
                    expect_ref[index - arrays + outputs, spot, width:] = moved
    for index, shock in enumerate(shocks):
        responses[index, :, width:] = tails_ref[shock]
    partial_sums(shocks, expect_ref, direct_ref, keep_ref, give_ref, responses, products)


def next_kernel(width, begins, shocks, direct_ref, expect_ref, tails_ref, *refs):
    messages = refs[: len(begins)]
    keep_ref, give_ref, responses, products = refs[len(begins) :]
    rows = messages[0].shape[0]
    z = lax.axis_index("hrow")
    for index, shock in enumerate(shocks):
        for mask, (ref, begin) in enumerate(zip(messages, begins)):
            column = begin + index * width
            responses[index, place(z, mask, rows), :width] = ref[:, column : column + width]
        responses[index, :, width:] = tails_ref[shock]
    partial_sums(shocks, expect_ref, direct_ref, keep_ref, give_ref, responses, products)


def size_of(leaf):
    shape = leaf.shape[:-1] + (-(-leaf.shape[-1] // LANES) * LANES,)
    return math.prod(shape) * leaf.dtype.itemsize


def call(kernel, name, out_shape, arrays, scratch=(), scalars=(), flops=0):
    held = sum(size_of(leaf) for leaf in jax.tree.leaves((arrays, out_shape)))
    taken = held + sum(size_of(leaf) for leaf in scratch if isinstance(leaf, jax.ShapeDtypeStruct) or jnp.issubdtype(leaf.dtype, jnp.number))
    return pl.pallas_call(
        kernel,
        name=name,
        out_shape=out_shape,
        in_specs=[pl.BlockSpec(memory_space=pltpu.SMEM)] * len(scalars)
        + [pl.BlockSpec(memory_space=pltpu.VMEM)] * len(arrays),
        out_specs=jax.tree.map(lambda _: pl.BlockSpec(memory_space=pltpu.VMEM), out_shape),
        scratch_shapes=scratch,
        cost_estimate=pl.CostEstimate(flops=flops, bytes_accessed=held, transcendentals=0),
        compiler_params=pltpu.CompilerParams(vmem_limit_bytes=taken * 3 // 2 + (4 << 20)),
    )(*scalars, *arrays)


def shards(expect, distrib, direct, pair_index):
    planes = lax.axis_size("hrow")
    col_devices = lax.axis_size("hcol")
    chips = col_devices // 2
    outputs, rows, grid = expect.shape
    shocks = distrib.shape[0]
    horizon = rows * planes
    cols = horizon // col_devices
    pairs = pair_index.shape[0]
    width = grid // LANES // planes * LANES
    rest = grid - width * planes
    depth = width + rest
    share = packed_share(planes, outputs + shocks, rest)
    near = planes // 2
    masks = range(1, planes)

    def cut(name, arrays, sent, counts, tail_at=None):
        def columns(m, count):
            if tail_at is None or share:
                return count * width + (0 if tail_at is None else LANES)
            return count * width + (len(arrays) if m == 0 else len(arrays) - tail_at) * rest

        return call(
            functools.partial(cut_kernel, width, planes, sent, counts, tail_at),
            name,
            [jax.ShapeDtypeStruct((rows, columns(m, count)), expect.dtype) for m, count in zip(sent, counts)],
            arrays,
            [pltpu.SemaphoreType.DMA((sum(counts) + len(sent) * len(arrays),))],
        )

    def to_planes(messages, sent):
        return [swap(message, "hrow", m) if m else message for m, message in zip(sent, messages)]

    z = lax.axis_index("hrow")
    chip = lax.axis_index("hcol") // 2
    flat = direct.reshape(shocks * outputs, cols, 1)

    def kernel_call(kernel, name, group, arrays, extra=()):
        part = jax.ShapeDtypeStruct((chips, planes, len(group), cols, outputs * rows), jnp.float32)
        return call(
            kernel,
            name,
            (*extra, part, part),
            arrays,
            [
                pltpu.VMEM((len(group), horizon, depth), distrib.dtype),
                pltpu.VMEM((outputs, horizon, horizon), jnp.float32),
            ],
            flops=2 * len(group) * outputs * horizon * horizon * depth,
        )

    def over_chips(values, begin):
        def block(index):
            parts = [lax.dynamic_slice_in_dim(value, begin, near, axis=1) for value in values]
            return jnp.concatenate([lax.dynamic_index_in_dim(part, index, 0, False) for part in parts], axis=1)

        swaps = [swap(block(chip ^ m), "hcol", 2 * m) for m in range(chips - 1, 0, -1)]
        return functools.reduce(jnp.add, [block(chip)] + swaps)

    def over_cores(keep, give):
        return keep + swap(give, "hcol", 1)

    group = range(FIRST)
    rest_group = range(FIRST, shocks)
    arrays = [expect[o] for o in range(outputs)] + [distrib[s] for s in range(shocks)]
    some = outputs + len(group)
    counts = [len(arrays)] + [some] * (planes - 1)
    first = to_planes(cut("cut_0", arrays, range(planes), counts, outputs), range(planes))
    if rest_group:
        later = cut("cut_1", arrays[some:], masks, [len(rest_group)] * len(masks))
        later = first[:1] + to_planes(later, masks)
    expect_all, tails, *parts = kernel_call(
        functools.partial(first_kernel, width, planes, counts, group),
        "partial_0",
        group,
        [flat] + first[::-1],
        [
            jax.ShapeDtypeStruct((outputs, horizon, depth), expect.dtype),
            jax.ShapeDtypeStruct((shocks, horizon, rest), distrib.dtype),
        ],
    )
    sums = [over_cores(*parts)]
    if rest_group:
        begins = [some * width] + [0] * len(masks)
        parts = kernel_call(
            functools.partial(next_kernel, width, begins, rest_group),
            "partial_1",
            rest_group,
            [flat, expect_all, tails] + later,
        )
        sums.append(over_cores(*parts))

    here = z // near * near
    far_sum = over_chips(sums, planes - near - here)
    near_sum = over_chips(sums, here)

    def of_plane(m):
        return lax.dynamic_index_in_dim(far_sum if m >= near else near_sum, (z ^ m) % near, 0, False)

    far_total = functools.reduce(jnp.add, [swap(of_plane(m), "hrow", m) for m in range(near, planes)])
    far_total = lax.optimization_barrier(far_total)
    total = functools.reduce(
        jnp.add, [far_total, of_plane(0)] + [swap(of_plane(m), "hrow", m) for m in range(1, near)]
    )
    shock_of = pair_index[:, 0, None, None]
    output_of = pair_index[:, 1, None, None]
    picked = jnp.zeros((pairs, cols, rows), jnp.float32)
    for s in range(shocks):
        for o in range(outputs):
            one = total[s, :, o * rows : (o + 1) * rows]
            picked = jnp.where((shock_of == s) & (output_of == o), one, picked)
    return jnp.swapaxes(picked, 1, 2)


def solution(mesh):
    placed = (P(None, "hrow", "hcol"), P(None, "hrow", "hcol"), P(None, None, "hcol"), P())
    return jax.shard_map(
        shards, mesh=mesh, in_specs=placed, out_specs=P(None, "hrow", "hcol"), check_vma=False
    )
```

```python
import functools
import math

import jax
import jax.numpy as jnp
from jax import lax
from jax.experimental import pallas as pl
from jax.experimental.pallas import tpu as pltpu
from jax.sharding import PartitionSpec as P

LANES = 128
FIRST = 1


def swap(block, axis, mask):
    return lax.ppermute(block, axis, [(i, i ^ mask) for i in range(lax.axis_size(axis))])


def add_diagonals(block):
    rows, dates = block.shape
    lane = lax.broadcasted_iota(jnp.int32, (rows, LANES), 1)
    top_row = lax.broadcasted_iota(jnp.int32, (8, LANES), 0)
    tiles = [block[:, start : start + LANES] for start in range(0, dates, LANES)]
    offset = 1
    while offset < rows:
        moved = tiles
        if offset % LANES:
            turned = [pltpu.roll(tile, offset % LANES, 1) for tile in tiles]
            behind = [jnp.zeros_like(turned[0])] + turned[:-1]
            moved = [jnp.where(lane < offset % LANES, low, high) for low, high in zip(behind, turned)]
        past = offset // LANES
        sums = tiles[:past]
        for tile, more in zip(tiles[past:], moved[: len(tiles) - past]):
            if offset % 8:
                more = pltpu.roll(more, offset, 0)
                more = jnp.concatenate([jnp.where(top_row < offset, 0.0, more[:8]), more[8:]], axis=0)
                sums.append(tile + more)
            else:
                sums.append(jnp.concatenate([tile[:offset], tile[offset:] + more[: rows - offset]], axis=0))
        tiles = sums
        offset = offset * 2
    return jnp.concatenate(tiles, axis=1)


def packed_share(planes, arrays, rest):
    share = rest // planes
    return share if rest == LANES and share * arrays <= LANES and share * planes == rest else 0


def far_kernel(far, planes, count, *refs):
    pieces, ends, message = refs[:count], refs[count:-1], refs[-1]
    width = pieces[0].shape[1]
    for index, ref in enumerate(pieces):
        message[:, index * width : (index + 1) * width] = ref[...]
    tile = shared_tile([end[...] for end in ends], lax.axis_index("hrow") ^ far, ends[0].shape[1] // planes)
    message[:, count * width :] = tile.astype(message.dtype)


def shared_tile(ends, plane, share):
    spot = lax.broadcasted_iota(jnp.int32, ends[0].shape, 1)
    tile = jnp.zeros(ends[0].shape, jnp.float32)
    for index, end in enumerate(ends):
        shift = lax.rem(index * share + LANES - plane * share, LANES)
        inside = (spot >= index * share) & (spot < (index + 1) * share)
        tile = jnp.where(inside, pltpu.roll(end.astype(jnp.float32), shift, 1), tile)
    return tile


def cut_kernel(width, planes, masks, counts, tail_at, *refs):
    wholes = refs[: len(refs) - len(masks) - 1]
    *messages, sems = refs[len(wholes) :]
    rows, grid = messages[0].shape[0], wholes[0].shape[1]
    arrays = [ref.at[pl.ds(at, rows)] for ref in wholes for at in range(0, ref.shape[0], rows)]
    rest = grid - width * planes
    share = packed_share(planes, len(arrays), rest)
    z = lax.axis_index("hrow")
    copies = []

    def copy(source, begin, size, goal, column):
        part = source.at[:, pl.ds(begin, size)]
        copies.append(pltpu.make_async_copy(part, goal.at[:, pl.ds(column, size)], sems.at[len(copies)]))
        copies[-1].start()

    for message, mask, count in zip(messages, masks, counts):
        begin = pl.multiple_of((z ^ mask) * width, LANES)
        for index, source in enumerate(arrays[:count]):
            copy(source, begin, width, message, index * width)
        if tail_at is not None and not share:
            last = arrays[tail_at:] + (arrays[:tail_at] if mask == 0 else [])
            for index, source in enumerate(last):
                copy(source, grid - rest, rest, message, count * width + index * rest)
    if tail_at is not None and share:
        ends = [source[:, grid - rest :] for source in arrays]
        for message, mask, count in zip(messages, masks, counts):
            tile = shared_tile(ends, z ^ mask, share)
            message[:, count * width : count * width + LANES] = tile.astype(message.dtype)
    for one in copies:
        one.wait()


def partial_sums(shocks, expect_ref, direct_ref, keep_ref, give_ref, responses, products):
    outputs, horizon = products.shape[:2]
    chips, planes, _, half, lanes = keep_ref.shape
    width = lanes // outputs
    step = min(horizon, 256)
    z = lax.axis_index("hrow")
    c = lax.axis_index("hcol")
    core = c % 2
    mine = pl.ds(pl.multiple_of(c * half, half), half)
    first = lax.broadcasted_iota(jnp.int32, (half, LANES), 1) == 0
    for index, shock in enumerate(shocks):
        for output in range(outputs):
            for start in range(0, horizon, step):
                products[output, start : start + step, :] = lax.dot_general(
                    responses[index, start : start + step, :],
                    expect_ref[output],
                    (((1,), (1,)), ((), ())),
                    preferred_element_type=jnp.float32,
                )
            added = jnp.where(first & (z == 0), direct_ref[shock * outputs + output], 0.0)
            products[output, mine, :LANES] = products[output, mine, :LANES] + added
        last = [None] * outputs
        for start in range(0, horizon, step):
            blocks = []
            for output in range(outputs):
                block = add_diagonals(products[output, start : start + step, :])
                if last[output] is not None:
                    spread = jnp.broadcast_to(last[output], block.shape)
                    moved = pltpu.roll(spread, 1, 1, stride=1, stride_axis=0)
                    row_id = lax.broadcasted_iota(jnp.int32, block.shape, 0)
                    date_id = lax.broadcasted_iota(jnp.int32, block.shape, 1)
                    block = block + jnp.where(date_id > row_id, moved, 0.0)
                last[output] = block[step - 1 :]
                blocks.append(block)
            for plane in range(planes):
                dates = slice(plane * width, (plane + 1) * width)
                both = jnp.concatenate([block[:, dates] for block in blocks], axis=1)
                for part in range(step // (2 * half)):
                    low = both[2 * part * half : (2 * part + 1) * half]
                    high = both[(2 * part + 1) * half : (2 * part + 2) * half]
                    chip = start // (2 * half) + part
                    keep_ref[chip, plane, index] = jnp.where(core == 0, low, high)
                    give_ref[chip, plane, index] = jnp.where(core == 0, high, low)


def place(z, mask, rows):
    return pl.ds(pl.multiple_of((z ^ mask) * rows, rows), rows)


def first_kernel(width, planes, counts, shocks, direct_ref, *refs):
    messages = refs[:planes][::-1]
    expect_ref, tails_ref, keep_ref, give_ref, responses, products = refs[planes:]
    outputs = expect_ref.shape[0]
    rows = messages[0].shape[0]
    rest = tails_ref.shape[2]
    arrays = outputs + tails_ref.shape[0]
    share = packed_share(planes, arrays, rest)
    z = lax.axis_index("hrow")
    inside = lax.broadcasted_iota(jnp.int32, (rows, rest), 1) < share
    if not share:
        expect_ref[:, :, width:] = jnp.zeros_like(expect_ref[:, :, width:])
    for mask, (ref, count) in enumerate(zip(messages, counts)):
        spot = place(z, mask, rows)
        for o in range(outputs):
            expect_ref[o, spot, :width] = ref[:, o * width : (o + 1) * width]
        for index in range(len(shocks)):
            responses[index, spot, :width] = ref[:, (outputs + index) * width : (outputs + index + 1) * width]
        tail = count * width
        if share:
            tile = ref[:, tail : tail + rest].astype(jnp.float32)
            for index in range(arrays):
                moved = tile if index == 0 else pltpu.roll(tile, LANES - index * share, 1)
                moved = jnp.where(inside, moved, 0.0).astype(ref.dtype)
                if index < outputs:
                    expect_ref[index, spot, width:] = moved
                else:
                    tails_ref[index - outputs, spot, :] = moved
        else:
            for index in range(arrays if mask == 0 else arrays - outputs):
                moved = ref[:, tail + index * rest : tail + (index + 1) * rest]
                if index < arrays - outputs:
                    tails_ref[index, spot, :] = moved
                else:
                    expect_ref[index - arrays + outputs, spot, width:] = moved
    for index, shock in enumerate(shocks):
        responses[index, :, width:] = tails_ref[shock]
    partial_sums(shocks, expect_ref, direct_ref, keep_ref, give_ref, responses, products)


def next_kernel(width, begins, shocks, direct_ref, expect_ref, tails_ref, *refs):
    messages = refs[: len(begins)]
    keep_ref, give_ref, responses, products = refs[len(begins) :]
    rows = messages[0].shape[0]
    z = lax.axis_index("hrow")
    for index, shock in enumerate(shocks):
        for mask, (ref, begin) in enumerate(zip(messages, begins)):
            column = begin + index * width
            responses[index, place(z, mask, rows), :width] = ref[:, column : column + width]
        responses[index, :, width:] = tails_ref[shock]
    partial_sums(shocks, expect_ref, direct_ref, keep_ref, give_ref, responses, products)


def size_of(leaf):
    shape = leaf.shape[:-1] + (-(-leaf.shape[-1] // LANES) * LANES,)
    return math.prod(shape) * leaf.dtype.itemsize


def call(kernel, name, out_shape, arrays, scratch=(), scalars=(), flops=0):
    held = sum(size_of(leaf) for leaf in jax.tree.leaves((arrays, out_shape)))
    taken = held + sum(size_of(leaf) for leaf in scratch if isinstance(leaf, jax.ShapeDtypeStruct) or jnp.issubdtype(leaf.dtype, jnp.number))
    return pl.pallas_call(
        kernel,
        name=name,
        out_shape=out_shape,
        in_specs=[pl.BlockSpec(memory_space=pltpu.SMEM)] * len(scalars)
        + [pl.BlockSpec(memory_space=pltpu.VMEM)] * len(arrays),
        out_specs=jax.tree.map(lambda _: pl.BlockSpec(memory_space=pltpu.VMEM), out_shape),
        scratch_shapes=scratch,
        cost_estimate=pl.CostEstimate(flops=flops, bytes_accessed=held, transcendentals=0),
        compiler_params=pltpu.CompilerParams(vmem_limit_bytes=taken * 3 // 2 + (4 << 20)),
    )(*scalars, *arrays)


def shards(expect, distrib, direct, pair_index):
    planes = lax.axis_size("hrow")
    col_devices = lax.axis_size("hcol")
    chips = col_devices // 2
    outputs, rows, grid = expect.shape
    shocks = distrib.shape[0]
    horizon = rows * planes
    cols = horizon // col_devices
    pairs = pair_index.shape[0]
    width = grid // LANES // planes * LANES
    rest = grid - width * planes
    depth = width + rest
    share = packed_share(planes, outputs + shocks, rest)
    near = planes // 2
    masks = range(1, planes)

    def cut(name, arrays, sent, counts, tail_at=None):
        def columns(m, count):
            if tail_at is None or share:
                return count * width + (0 if tail_at is None else LANES)
            return count * width + (outputs + shocks if m == 0 else outputs + shocks - tail_at) * rest

        return call(
            functools.partial(cut_kernel, width, planes, sent, counts, tail_at),
            name,
            [jax.ShapeDtypeStruct((rows, columns(m, count)), expect.dtype) for m, count in zip(sent, counts)],
            arrays,
            [pltpu.SemaphoreType.DMA((sum(counts) + len(sent) * (outputs + shocks),))],
        )

    def to_planes(messages, sent):
        return [swap(message, "hrow", m) if m else message for m, message in zip(sent, messages)]

    z = lax.axis_index("hrow")
    chip = lax.axis_index("hcol") // 2
    flat = direct.reshape(shocks * outputs, cols, 1)

    def kernel_call(kernel, name, group, arrays, extra=()):
        part = jax.ShapeDtypeStruct((chips, planes, len(group), cols, outputs * rows), jnp.float32)
        return call(
            kernel,
            name,
            (*extra, part, part),
            arrays,
            [
                pltpu.VMEM((len(group), horizon, depth), distrib.dtype),
                pltpu.VMEM((outputs, horizon, horizon), jnp.float32),
            ],
            flops=2 * len(group) * outputs * horizon * horizon * depth,
        )

    def over_chips(values, begin):
        def block(index):
            parts = [lax.dynamic_slice_in_dim(value, begin, near, axis=1) for value in values]
            return jnp.concatenate([lax.dynamic_index_in_dim(part, index, 0, False) for part in parts], axis=1)

        swaps = [swap(block(chip ^ m), "hcol", 2 * m) for m in range(chips - 1, 0, -1)]
        return functools.reduce(jnp.add, [block(chip)] + swaps)

    def over_cores(keep, give):
        return keep + swap(give, "hcol", 1)

    group = range(FIRST)
    rest_group = range(FIRST, shocks)
    some = outputs + len(group)
    counts = [outputs + shocks] + [some] * (planes - 1)
    sent = list(range(planes))
    alone = []
    arrays = [expect[o] for o in range(outputs)] + [distrib[s] for s in range(shocks)]
    if share:
        far = sent.pop()
        begin = (z ^ far) * width
        message = call(
            functools.partial(far_kernel, far, planes, some),
            "cut_far",
            jax.ShapeDtypeStruct((rows, some * width + rest), expect.dtype),
            [lax.dynamic_slice_in_dim(one, begin, width, 1) for one in arrays[:some]]
            + [one[:, grid - rest :] for one in arrays],
        )
        expect, distrib, message = lax.optimization_barrier((expect, distrib, message))
        alone = [message]
    arrays = [expect[o] for o in range(outputs)] + [distrib[s] for s in range(shocks)]
    whole = [expect.reshape(outputs * rows, grid)] + arrays[outputs:]
    first = to_planes([*cut("cut_0", whole, sent, counts[: len(sent)], outputs), *alone], range(planes))
    if rest_group:
        later = cut("cut_1", arrays[some:], masks, [len(rest_group)] * len(masks))
        later = first[:1] + to_planes(later, masks)
    expect_all, tails, *parts = kernel_call(
        functools.partial(first_kernel, width, planes, counts, group),
        "partial_0",
        group,
        [flat] + first[::-1],
        [
            jax.ShapeDtypeStruct((outputs, horizon, depth), expect.dtype),
            jax.ShapeDtypeStruct((shocks, horizon, rest), distrib.dtype),
        ],
    )
    sums = [over_cores(*parts)]
    if rest_group:
        begins = [some * width] + [0] * len(masks)
        parts = kernel_call(
            functools.partial(next_kernel, width, begins, rest_group),
            "partial_1",
            rest_group,
            [flat, expect_all, tails] + later,
        )
        sums.append(over_cores(*parts))

    here = z // near * near
    far_sum = over_chips(sums, planes - near - here)
    near_sum = over_chips(sums, here)

    def of_plane(m):
        return lax.dynamic_index_in_dim(far_sum if m >= near else near_sum, (z ^ m) % near, 0, False)

    far_total = functools.reduce(jnp.add, [swap(of_plane(m), "hrow", m) for m in range(near, planes)])
    far_total = lax.optimization_barrier(far_total)
    total = functools.reduce(
        jnp.add, [far_total, of_plane(0)] + [swap(of_plane(m), "hrow", m) for m in range(1, near)]
    )
    shock_of = pair_index[:, 0, None, None]
    output_of = pair_index[:, 1, None, None]
    picked = jnp.zeros((pairs, cols, rows), jnp.float32)
    for s in range(shocks):
        for o in range(outputs):
            one = total[s, :, o * rows : (o + 1) * rows]
            picked = jnp.where((shock_of == s) & (output_of == o), one, picked)
    return jnp.swapaxes(picked, 1, 2)


def solution(mesh):
    placed = (P(None, "hrow", "hcol"), P(None, "hrow", "hcol"), P(None, None, "hcol"), P())
    return jax.shard_map(
        shards, mesh=mesh, in_specs=placed, out_specs=P(None, "hrow", "hcol"), check_vma=False
    )
```

```python
import functools
import math

import jax
import jax.numpy as jnp
from jax import lax
from jax.experimental import pallas as pl
from jax.experimental.pallas import tpu as pltpu
from jax.sharding import PartitionSpec as P

LANES = 128
FIRST = 1


def swap(block, axis, mask):
    return lax.ppermute(block, axis, [(i, i ^ mask) for i in range(lax.axis_size(axis))])


def add_diagonals(block):
    rows, dates = block.shape
    lane = lax.broadcasted_iota(jnp.int32, (rows, LANES), 1)
    top_row = lax.broadcasted_iota(jnp.int32, (8, LANES), 0)
    tiles = [block[:, start : start + LANES] for start in range(0, dates, LANES)]
    offset = 1
    while offset < rows:
        moved = tiles
        if offset % LANES:
            turned = [pltpu.roll(tile, offset % LANES, 1) for tile in tiles]
            behind = [jnp.zeros_like(turned[0])] + turned[:-1]
            moved = [jnp.where(lane < offset % LANES, low, high) for low, high in zip(behind, turned)]
        past = offset // LANES
        sums = tiles[:past]
        for tile, more in zip(tiles[past:], moved[: len(tiles) - past]):
            if offset % 8:
                more = pltpu.roll(more, offset, 0)
                more = jnp.concatenate([jnp.where(top_row < offset, 0.0, more[:8]), more[8:]], axis=0)
                sums.append(tile + more)
            else:
                sums.append(jnp.concatenate([tile[:offset], tile[offset:] + more[: rows - offset]], axis=0))
        tiles = sums
        offset = offset * 2
    return jnp.concatenate(tiles, axis=1)


def packed_share(planes, arrays, rest):
    share = rest // planes
    return share if rest == LANES and share * arrays <= LANES and share * planes == rest else 0


def far_kernel(far, planes, count, *refs):
    pieces, ends, message = refs[:count], refs[count:-1], refs[-1]
    width = pieces[0].shape[1]
    for index, ref in enumerate(pieces):
        message[:, index * width : (index + 1) * width] = ref[...]
    tile = shared_tile([end[...] for end in ends], lax.axis_index("hrow") ^ far, ends[0].shape[1] // planes)
    message[:, count * width :] = tile.astype(message.dtype)


def shared_tile(ends, plane, share):
    spot = lax.broadcasted_iota(jnp.int32, ends[0].shape, 1)
    tile = jnp.zeros(ends[0].shape, jnp.float32)
    for index, end in enumerate(ends):
        shift = lax.rem(index * share + LANES - plane * share, LANES)
        inside = (spot >= index * share) & (spot < (index + 1) * share)
        tile = jnp.where(inside, pltpu.roll(end.astype(jnp.float32), shift, 1), tile)
    return tile


def cut_kernel(width, planes, masks, counts, tail_at, *refs):
    wholes = refs[: len(refs) - len(masks) - 1]
    *messages, sems = refs[len(wholes) :]
    rows, grid = messages[0].shape[0], wholes[0].shape[1]
    arrays = [ref.at[pl.ds(at, rows)] for ref in wholes for at in range(0, ref.shape[0], rows)]
    rest = grid - width * planes
    share = packed_share(planes, len(arrays), rest)
    z = lax.axis_index("hrow")
    copies = []

    def copy(source, begin, size, goal, column):
        part = source.at[:, pl.ds(begin, size)]
        copies.append(pltpu.make_async_copy(part, goal.at[:, pl.ds(column, size)], sems.at[len(copies)]))
        copies[-1].start()

    for message, mask, count in zip(messages, masks, counts):
        begin = pl.multiple_of((z ^ mask) * width, LANES)
        for index, source in enumerate(arrays[:count]):
            copy(source, begin, width, message, index * width)
        if tail_at is not None and not share:
            last = arrays[tail_at:] + (arrays[:tail_at] if mask == 0 else [])
            for index, source in enumerate(last):
                copy(source, grid - rest, rest, message, count * width + index * rest)
    if tail_at is not None and share:
        ends = [source[:, grid - rest :] for source in arrays]
        for message, mask, count in zip(messages, masks, counts):
            tile = shared_tile(ends, z ^ mask, share)
            message[:, count * width : count * width + LANES] = tile.astype(message.dtype)
    for one in copies:
        one.wait()


def partial_sums(shocks, expect_ref, direct_ref, parts, responses, products):
    outputs, horizon = products.shape[:2]
    chips, near, _, half, lanes = parts[0].shape
    planes = 2 * near
    width = lanes // outputs
    step = min(horizon, 256)
    z = lax.axis_index("hrow")
    c = lax.axis_index("hcol")
    core = c % 2
    mine = pl.ds(pl.multiple_of(c * half, half), half)
    first = lax.broadcasted_iota(jnp.int32, (half, LANES), 1) == 0
    for index, shock in enumerate(shocks):
        for output in range(outputs):
            for start in range(0, horizon, step):
                products[output, start : start + step, :] = lax.dot_general(
                    responses[index, start : start + step, :],
                    expect_ref[output],
                    (((1,), (1,)), ((), ())),
                    preferred_element_type=jnp.float32,
                )
            added = jnp.where(first & (z == 0), direct_ref[shock * outputs + output], 0.0)
            products[output, mine, :LANES] = products[output, mine, :LANES] + added
        last = [None] * outputs
        for start in range(0, horizon, step):
            blocks = []
            for output in range(outputs):
                block = add_diagonals(products[output, start : start + step, :])
                if last[output] is not None:
                    spread = jnp.broadcast_to(last[output], block.shape)
                    moved = pltpu.roll(spread, 1, 1, stride=1, stride_axis=0)
                    row_id = lax.broadcasted_iota(jnp.int32, block.shape, 0)
                    date_id = lax.broadcasted_iota(jnp.int32, block.shape, 1)
                    block = block + jnp.where(date_id > row_id, moved, 0.0)
                last[output] = block[step - 1 :]
                blocks.append(block)
            both = []
            for plane in range(planes):
                dates = slice(plane * width, (plane + 1) * width)
                both.append(jnp.concatenate([block[:, dates] for block in blocks], axis=1))
            for plane in range(near):
                far = jnp.where(z < near, both[near + plane], both[plane])
                here = jnp.where(z < near, both[plane], both[near + plane])
                for side, block in enumerate((far, here)):
                    for part in range(step // (2 * half)):
                        low = block[2 * part * half : (2 * part + 1) * half]
                        high = block[(2 * part + 1) * half : (2 * part + 2) * half]
                        chip = start // (2 * half) + part
                        parts[2 * side][chip, plane, index] = jnp.where(core == 0, low, high)
                        parts[2 * side + 1][chip, plane, index] = jnp.where(core == 0, high, low)


def place(z, mask, rows):
    return pl.ds(pl.multiple_of((z ^ mask) * rows, rows), rows)


def first_kernel(width, planes, counts, shocks, direct_ref, *refs):
    messages = refs[:planes][::-1]
    expect_ref, tails_ref, *parts, responses, products = refs[planes:]
    outputs = expect_ref.shape[0]
    rows = messages[0].shape[0]
    rest = tails_ref.shape[2]
    arrays = outputs + tails_ref.shape[0]
    share = packed_share(planes, arrays, rest)
    z = lax.axis_index("hrow")
    inside = lax.broadcasted_iota(jnp.int32, (rows, rest), 1) < share
    if not share:
        expect_ref[:, :, width:] = jnp.zeros_like(expect_ref[:, :, width:])
    for mask, (ref, count) in enumerate(zip(messages, counts)):
        spot = place(z, mask, rows)
        for o in range(outputs):
            expect_ref[o, spot, :width] = ref[:, o * width : (o + 1) * width]
        for index in range(len(shocks)):
            responses[index, spot, :width] = ref[:, (outputs + index) * width : (outputs + index + 1) * width]
        tail = count * width
        if share:
            tile = ref[:, tail : tail + rest].astype(jnp.float32)
            for index in range(arrays):
                moved = tile if index == 0 else pltpu.roll(tile, LANES - index * share, 1)
                moved = jnp.where(inside, moved, 0.0).astype(ref.dtype)
                if index < outputs:
                    expect_ref[index, spot, width:] = moved
                else:
                    tails_ref[index - outputs, spot, :] = moved
        else:
            for index in range(arrays if mask == 0 else arrays - outputs):
                moved = ref[:, tail + index * rest : tail + (index + 1) * rest]
                if index < arrays - outputs:
                    tails_ref[index, spot, :] = moved
                else:
                    expect_ref[index - arrays + outputs, spot, width:] = moved
    for index, shock in enumerate(shocks):
        responses[index, :, width:] = tails_ref[shock]
    partial_sums(shocks, expect_ref, direct_ref, parts, responses, products)


def next_kernel(width, begins, shocks, direct_ref, expect_ref, tails_ref, *refs):
    messages = refs[: len(begins)]
    *parts, responses, products = refs[len(begins) :]
    rows = messages[0].shape[0]
    z = lax.axis_index("hrow")
    for index, shock in enumerate(shocks):
        for mask, (ref, begin) in enumerate(zip(messages, begins)):
            column = begin + index * width
            responses[index, place(z, mask, rows), :width] = ref[:, column : column + width]
        responses[index, :, width:] = tails_ref[shock]
    partial_sums(shocks, expect_ref, direct_ref, parts, responses, products)


def size_of(leaf):
    shape = leaf.shape[:-1] + (-(-leaf.shape[-1] // LANES) * LANES,)
    return math.prod(shape) * leaf.dtype.itemsize


def call(kernel, name, out_shape, arrays, scratch=(), scalars=(), flops=0):
    held = sum(size_of(leaf) for leaf in jax.tree.leaves((arrays, out_shape)))
    taken = held + sum(size_of(leaf) for leaf in scratch if isinstance(leaf, jax.ShapeDtypeStruct) or jnp.issubdtype(leaf.dtype, jnp.number))
    return pl.pallas_call(
        kernel,
        name=name,
        out_shape=out_shape,
        in_specs=[pl.BlockSpec(memory_space=pltpu.SMEM)] * len(scalars)
        + [pl.BlockSpec(memory_space=pltpu.VMEM)] * len(arrays),
        out_specs=jax.tree.map(lambda _: pl.BlockSpec(memory_space=pltpu.VMEM), out_shape),
        scratch_shapes=scratch,
        cost_estimate=pl.CostEstimate(flops=flops, bytes_accessed=held, transcendentals=0),
        compiler_params=pltpu.CompilerParams(vmem_limit_bytes=taken * 3 // 2 + (4 << 20)),
    )(*scalars, *arrays)


def shards(expect, distrib, direct, pair_index):
    planes = lax.axis_size("hrow")
    col_devices = lax.axis_size("hcol")
    chips = col_devices // 2
    outputs, rows, grid = expect.shape
    shocks = distrib.shape[0]
    horizon = rows * planes
    cols = horizon // col_devices
    pairs = pair_index.shape[0]
    width = grid // LANES // planes * LANES
    rest = grid - width * planes
    depth = width + rest
    share = packed_share(planes, outputs + shocks, rest)
    near = planes // 2
    masks = range(1, planes)

    def cut(name, arrays, sent, counts, tail_at=None):
        def columns(m, count):
            if tail_at is None or share:
                return count * width + (0 if tail_at is None else LANES)
            return count * width + (outputs + shocks if m == 0 else outputs + shocks - tail_at) * rest

        return call(
            functools.partial(cut_kernel, width, planes, sent, counts, tail_at),
            name,
            [jax.ShapeDtypeStruct((rows, columns(m, count)), expect.dtype) for m, count in zip(sent, counts)],
            arrays,
            [pltpu.SemaphoreType.DMA((sum(counts) + len(sent) * (outputs + shocks),))],
        )

    def to_planes(messages, sent):
        return [swap(message, "hrow", m) if m else message for m, message in zip(sent, messages)]

    z = lax.axis_index("hrow")
    chip = lax.axis_index("hcol") // 2
    flat = direct.reshape(shocks * outputs, cols, 1)

    def kernel_call(kernel, name, group, arrays, extra=()):
        part = jax.ShapeDtypeStruct((chips, near, len(group), cols, outputs * rows), jnp.float32)
        return call(
            kernel,
            name,
            (*extra, part, part, part, part),
            arrays,
            [
                pltpu.VMEM((len(group), horizon, depth), distrib.dtype),
                pltpu.VMEM((outputs, horizon, horizon), jnp.float32),
            ],
            flops=2 * len(group) * outputs * horizon * horizon * depth,
        )

    def over_cores(far_keep, far_give, near_keep, near_give):
        return far_keep + swap(far_give, "hcol", 1), near_keep + swap(near_give, "hcol", 1)

    def over_chips(values):
        def block(index):
            return jnp.concatenate([lax.dynamic_index_in_dim(one, index, 0, False) for one in values], axis=1)

        swaps = [swap(block(chip ^ m), "hcol", 2 * m) for m in range(chips - 1, 0, -1)]
        return functools.reduce(jnp.add, [block(chip)] + swaps)

    group = range(FIRST)
    rest_group = range(FIRST, shocks)
    some = outputs + len(group)
    counts = [outputs + shocks] + [some] * (planes - 1)
    sent = list(range(planes))
    alone = []
    arrays = [expect[o] for o in range(outputs)] + [distrib[s] for s in range(shocks)]
    if share:
        far = sent.pop()
        begin = (z ^ far) * width
        message = call(
            functools.partial(far_kernel, far, planes, some),
            "cut_far",
            jax.ShapeDtypeStruct((rows, some * width + rest), expect.dtype),
            [lax.dynamic_slice_in_dim(one, begin, width, 1) for one in arrays[:some]]
            + [one[:, grid - rest :] for one in arrays],
        )
        expect, distrib, message = lax.optimization_barrier((expect, distrib, message))
        alone = [message]
    arrays = [expect[o] for o in range(outputs)] + [distrib[s] for s in range(shocks)]
    whole = [expect.reshape(outputs * rows, grid)] + arrays[outputs:]
    first = to_planes([*cut("cut_0", whole, sent, counts[: len(sent)], outputs), *alone], range(planes))
    if rest_group:
        later = cut("cut_1", arrays[some:], masks, [len(rest_group)] * len(masks))
        later = first[:1] + to_planes(later, masks)
    expect_all, tails, *parts = kernel_call(
        functools.partial(first_kernel, width, planes, counts, group),
        "partial_0",
        group,
        [flat] + first[::-1],
        [
            jax.ShapeDtypeStruct((outputs, horizon, depth), expect.dtype),
            jax.ShapeDtypeStruct((shocks, horizon, rest), distrib.dtype),
        ],
    )
    sums = [over_cores(*parts)]
    if rest_group:
        begins = [some * width] + [0] * len(masks)
        parts = kernel_call(
            functools.partial(next_kernel, width, begins, rest_group),
            "partial_1",
            rest_group,
            [flat, expect_all, tails] + later,
        )
        sums.append(over_cores(*parts))

    far_sum, near_sum = (over_chips(values) for values in zip(*sums))

    def of_plane(m):
        return lax.dynamic_index_in_dim(far_sum if m >= near else near_sum, (z ^ m) % near, 0, False)

    far_total = functools.reduce(jnp.add, [swap(of_plane(m), "hrow", m) for m in range(near, planes)])
    far_total = lax.optimization_barrier(far_total)
    total = functools.reduce(
        jnp.add, [far_total, of_plane(0)] + [swap(of_plane(m), "hrow", m) for m in range(1, near)]
    )
    shock_of = pair_index[:, 0, None, None]
    output_of = pair_index[:, 1, None, None]
    picked = jnp.zeros((pairs, cols, rows), jnp.float32)
    for s in range(shocks):
        for o in range(outputs):
            one = total[s, :, o * rows : (o + 1) * rows]
            picked = jnp.where((shock_of == s) & (output_of == o), one, picked)
    return jnp.swapaxes(picked, 1, 2)


def solution(mesh):
    placed = (P(None, "hrow", "hcol"), P(None, "hrow", "hcol"), P(None, None, "hcol"), P())
    return jax.shard_map(
        shards, mesh=mesh, in_specs=placed, out_specs=P(None, "hrow", "hcol"), check_vma=False
    )
```

```python
import functools
import math

import jax
import jax.numpy as jnp
from jax import lax
from jax.experimental import pallas as pl
from jax.experimental.pallas import tpu as pltpu
from jax.sharding import PartitionSpec as P

LANES = 128
FIRST = 1


def swap(block, axis, mask):
    return lax.ppermute(block, axis, [(i, i ^ mask) for i in range(lax.axis_size(axis))])


def add_diagonals(block):
    rows, dates = block.shape
    lane = lax.broadcasted_iota(jnp.int32, (rows, LANES), 1)
    top_row = lax.broadcasted_iota(jnp.int32, (8, LANES), 0)
    tiles = [block[:, start : start + LANES] for start in range(0, dates, LANES)]
    offset = 1
    while offset < rows:
        moved = tiles
        if offset % LANES:
            turned = [pltpu.roll(tile, offset % LANES, 1) for tile in tiles]
            behind = [jnp.zeros_like(turned[0])] + turned[:-1]
            moved = [jnp.where(lane < offset % LANES, low, high) for low, high in zip(behind, turned)]
        past = offset // LANES
        sums = tiles[:past]
        for tile, more in zip(tiles[past:], moved[: len(tiles) - past]):
            if offset % 8:
                more = pltpu.roll(more, offset, 0)
                more = jnp.concatenate([jnp.where(top_row < offset, 0.0, more[:8]), more[8:]], axis=0)
                sums.append(tile + more)
            else:
                sums.append(jnp.concatenate([tile[:offset], tile[offset:] + more[: rows - offset]], axis=0))
        tiles = sums
        offset = offset * 2
    return jnp.concatenate(tiles, axis=1)


def packed_share(planes, arrays, rest):
    share = rest // planes
    return share if rest == LANES and share * arrays <= LANES and share * planes == rest else 0


def shared_tile(ends, plane, share):
    spot = lax.broadcasted_iota(jnp.int32, ends[0].shape, 1)
    tile = jnp.zeros(ends[0].shape, jnp.float32)
    for index, end in enumerate(ends):
        shift = lax.rem(index * share + LANES - plane * share, LANES)
        inside = (spot >= index * share) & (spot < (index + 1) * share)
        tile = jnp.where(inside, pltpu.roll(end.astype(jnp.float32), shift, 1), tile)
    return tile


def cut_kernel(width, planes, masks, counts, tail_at, *refs):
    wholes = refs[: len(refs) - len(masks) - 1]
    *messages, sems = refs[len(wholes) :]
    rows, grid = messages[0].shape[0], wholes[0].shape[1]
    arrays = [ref.at[pl.ds(at, rows)] for ref in wholes for at in range(0, ref.shape[0], rows)]
    rest = grid - width * planes
    share = packed_share(planes, len(arrays), rest)
    z = lax.axis_index("hrow")
    copies = []

    def copy(source, begin, size, goal, column):
        part = source.at[:, pl.ds(begin, size)]
        copies.append(pltpu.make_async_copy(part, goal.at[:, pl.ds(column, size)], sems.at[len(copies)]))
        copies[-1].start()

    for message, mask, count in zip(messages, masks, counts):
        begin = pl.multiple_of((z ^ mask) * width, LANES)
        for index, source in enumerate(arrays[:count]):
            copy(source, begin, width, message, index * width)
        if tail_at is not None and not share:
            last = arrays[tail_at:] + (arrays[:tail_at] if mask == 0 else [])
            for index, source in enumerate(last):
                copy(source, grid - rest, rest, message, count * width + index * rest)
    if tail_at is not None and share:
        ends = [source[:, grid - rest :] for source in arrays]
        for message, mask, count in zip(messages, masks, counts):
            tile = shared_tile(ends, z ^ mask, share)
            message[:, count * width : count * width + LANES] = tile.astype(message.dtype)
    for one in copies:
        one.wait()


def partial_sums(shocks, expect_ref, direct_ref, parts, responses, products):
    outputs, horizon = products.shape[:2]
    chips, near, _, half, lanes = parts[0].shape
    planes = 2 * near
    width = lanes // outputs
    step = min(horizon, 256)
    z = lax.axis_index("hrow")
    c = lax.axis_index("hcol")
    core = c % 2
    mine = pl.ds(pl.multiple_of(c * half, half), half)
    first = lax.broadcasted_iota(jnp.int32, (half, LANES), 1) == 0
    for index, shock in enumerate(shocks):
        for output in range(outputs):
            for start in range(0, horizon, step):
                products[output, start : start + step, :] = lax.dot_general(
                    responses[index, start : start + step, :],
                    expect_ref[output],
                    (((1,), (1,)), ((), ())),
                    preferred_element_type=jnp.float32,
                )
            added = jnp.where(first & (z == 0), direct_ref[shock * outputs + output], 0.0)
            products[output, mine, :LANES] = products[output, mine, :LANES] + added
        last = [None] * outputs
        for start in range(0, horizon, step):
            blocks = []
            for output in range(outputs):
                block = add_diagonals(products[output, start : start + step, :])
                if last[output] is not None:
                    spread = jnp.broadcast_to(last[output], block.shape)
                    moved = pltpu.roll(spread, 1, 1, stride=1, stride_axis=0)
                    row_id = lax.broadcasted_iota(jnp.int32, block.shape, 0)
                    date_id = lax.broadcasted_iota(jnp.int32, block.shape, 1)
                    block = block + jnp.where(date_id > row_id, moved, 0.0)
                last[output] = block[step - 1 :]
                blocks.append(block)
            both = []
            for plane in range(planes):
                dates = slice(plane * width, (plane + 1) * width)
                both.append(jnp.concatenate([block[:, dates] for block in blocks], axis=1))
            for plane in range(near):
                far = jnp.where(z < near, both[near + plane], both[plane])
                here = jnp.where(z < near, both[plane], both[near + plane])
                for side, block in enumerate((far, here)):
                    for part in range(step // (2 * half)):
                        low = block[2 * part * half : (2 * part + 1) * half]
                        high = block[(2 * part + 1) * half : (2 * part + 2) * half]
                        chip = start // (2 * half) + part
                        parts[2 * side][chip, plane, index] = jnp.where(core == 0, low, high)
                        parts[2 * side + 1][chip, plane, index] = jnp.where(core == 0, high, low)


def place(z, mask, rows):
    return pl.ds(pl.multiple_of((z ^ mask) * rows, rows), rows)


def first_kernel(width, planes, counts, shocks, direct_ref, *refs):
    messages = refs[:planes][::-1]
    expect_ref, tails_ref, *parts, responses, products = refs[planes:]
    outputs = expect_ref.shape[0]
    rows = messages[0].shape[0]
    rest = tails_ref.shape[2]
    arrays = outputs + tails_ref.shape[0]
    share = packed_share(planes, arrays, rest)
    z = lax.axis_index("hrow")
    inside = lax.broadcasted_iota(jnp.int32, (rows, rest), 1) < share
    if not share:
        expect_ref[:, :, width:] = jnp.zeros_like(expect_ref[:, :, width:])
    for mask, (ref, count) in enumerate(zip(messages, counts)):
        spot = place(z, mask, rows)
        for o in range(outputs):
            expect_ref[o, spot, :width] = ref[:, o * width : (o + 1) * width]
        for index in range(len(shocks)):
            responses[index, spot, :width] = ref[:, (outputs + index) * width : (outputs + index + 1) * width]
        tail = count * width
        if share:
            tile = ref[:, tail : tail + rest].astype(jnp.float32)
            for index in range(arrays):
                moved = tile if index == 0 else pltpu.roll(tile, LANES - index * share, 1)
                moved = jnp.where(inside, moved, 0.0).astype(ref.dtype)
                if index < outputs:
                    expect_ref[index, spot, width:] = moved
                else:
                    tails_ref[index - outputs, spot, :] = moved
        else:
            for index in range(arrays if mask == 0 else arrays - outputs):
                moved = ref[:, tail + index * rest : tail + (index + 1) * rest]
                if index < arrays - outputs:
                    tails_ref[index, spot, :] = moved
                else:
                    expect_ref[index - arrays + outputs, spot, width:] = moved
    for index, shock in enumerate(shocks):
        responses[index, :, width:] = tails_ref[shock]
    partial_sums(shocks, expect_ref, direct_ref, parts, responses, products)


def next_kernel(width, begins, shocks, direct_ref, expect_ref, tails_ref, *refs):
    messages = refs[: len(begins)]
    *parts, responses, products = refs[len(begins) :]
    rows = messages[0].shape[0]
    z = lax.axis_index("hrow")
    for index, shock in enumerate(shocks):
        for mask, (ref, begin) in enumerate(zip(messages, begins)):
            column = begin + index * width
            responses[index, place(z, mask, rows), :width] = ref[:, column : column + width]
        responses[index, :, width:] = tails_ref[shock]
    partial_sums(shocks, expect_ref, direct_ref, parts, responses, products)


def size_of(leaf):
    shape = leaf.shape[:-1] + (-(-leaf.shape[-1] // LANES) * LANES,)
    return math.prod(shape) * leaf.dtype.itemsize


def call(kernel, name, out_shape, arrays, scratch=(), scalars=(), flops=0):
    held = sum(size_of(leaf) for leaf in jax.tree.leaves((arrays, out_shape)))
    taken = held + sum(size_of(leaf) for leaf in scratch if isinstance(leaf, jax.ShapeDtypeStruct) or jnp.issubdtype(leaf.dtype, jnp.number))
    return pl.pallas_call(
        kernel,
        name=name,
        out_shape=out_shape,
        in_specs=[pl.BlockSpec(memory_space=pltpu.SMEM)] * len(scalars)
        + [pl.BlockSpec(memory_space=pltpu.VMEM)] * len(arrays),
        out_specs=jax.tree.map(lambda _: pl.BlockSpec(memory_space=pltpu.VMEM), out_shape),
        scratch_shapes=scratch,
        cost_estimate=pl.CostEstimate(flops=flops, bytes_accessed=held, transcendentals=0),
        compiler_params=pltpu.CompilerParams(vmem_limit_bytes=taken * 3 // 2 + (4 << 20)),
    )(*scalars, *arrays)


def shards(expect, distrib, direct, pair_index):
    planes = lax.axis_size("hrow")
    col_devices = lax.axis_size("hcol")
    chips = col_devices // 2
    outputs, rows, grid = expect.shape
    shocks = distrib.shape[0]
    horizon = rows * planes
    cols = horizon // col_devices
    pairs = pair_index.shape[0]
    width = grid // LANES // planes * LANES
    rest = grid - width * planes
    depth = width + rest
    share = packed_share(planes, outputs + shocks, rest)
    near = planes // 2
    masks = range(1, planes)

    def cut(name, arrays, sent, counts, tail_at=None):
        def columns(m, count):
            if tail_at is None or share:
                return count * width + (0 if tail_at is None else LANES)
            return count * width + (outputs + shocks if m == 0 else outputs + shocks - tail_at) * rest

        return call(
            functools.partial(cut_kernel, width, planes, sent, counts, tail_at),
            name,
            [jax.ShapeDtypeStruct((rows, columns(m, count)), expect.dtype) for m, count in zip(sent, counts)],
            arrays,
            [pltpu.SemaphoreType.DMA((sum(counts) + len(sent) * (outputs + shocks),))],
        )

    def to_planes(messages, sent):
        return [swap(message, "hrow", m) if m else message for m, message in zip(sent, messages)]

    z = lax.axis_index("hrow")
    chip = lax.axis_index("hcol") // 2
    flat = direct.reshape(shocks * outputs, cols, 1)

    def kernel_call(kernel, name, group, arrays, extra=()):
        part = jax.ShapeDtypeStruct((chips, near, len(group), cols, outputs * rows), jnp.float32)
        return call(
            kernel,
            name,
            (*extra, part, part, part, part),
            arrays,
            [
                pltpu.VMEM((len(group), horizon, depth), distrib.dtype),
                pltpu.VMEM((outputs, horizon, horizon), jnp.float32),
            ],
            flops=2 * len(group) * outputs * horizon * horizon * depth,
        )

    def over_cores(far_keep, far_give, near_keep, near_give):
        return far_keep + swap(far_give, "hcol", 1), near_keep + swap(near_give, "hcol", 1)

    def over_chips(values):
        def block(index):
            return jnp.concatenate([lax.dynamic_index_in_dim(one, index, 0, False) for one in values], axis=1)

        swaps = [swap(block(chip ^ m), "hcol", 2 * m) for m in range(chips - 1, 0, -1)]
        return functools.reduce(jnp.add, [block(chip)] + swaps)

    group = range(FIRST)
    rest_group = range(FIRST, shocks)
    some = outputs + len(group)
    counts = [outputs + shocks] + [some] * (planes - 1)
    sent = list(range(planes))
    alone = []
    arrays = [expect[o] for o in range(outputs)] + [distrib[s] for s in range(shocks)]
    whole = [expect.reshape(outputs * rows, grid)] + arrays[outputs:]
    (message,) = cut("cut_far", whole, sent[-1:], counts[-1:], outputs)
    whole, message = lax.optimization_barrier((whole, message))
    first = to_planes([*cut("cut_0", whole, sent[:-1], counts[:-1], outputs), message], range(planes))
    if rest_group:
        later = cut("cut_1", arrays[some:], masks, [len(rest_group)] * len(masks))
        later = first[:1] + to_planes(later, masks)
    expect_all, tails, *parts = kernel_call(
        functools.partial(first_kernel, width, planes, counts, group),
        "partial_0",
        group,
        [flat] + first[::-1],
        [
            jax.ShapeDtypeStruct((outputs, horizon, depth), expect.dtype),
            jax.ShapeDtypeStruct((shocks, horizon, rest), distrib.dtype),
        ],
    )
    sums = [over_cores(*parts)]
    if rest_group:
        begins = [some * width] + [0] * len(masks)
        parts = kernel_call(
            functools.partial(next_kernel, width, begins, rest_group),
            "partial_1",
            rest_group,
            [flat, expect_all, tails] + later,
        )
        sums.append(over_cores(*parts))

    far_sum, near_sum = (over_chips(values) for values in zip(*sums))

    def of_plane(m):
        return lax.dynamic_index_in_dim(far_sum if m >= near else near_sum, (z ^ m) % near, 0, False)

    far_total = functools.reduce(jnp.add, [swap(of_plane(m), "hrow", m) for m in range(near, planes)])
    far_total = lax.optimization_barrier(far_total)
    total = functools.reduce(
        jnp.add, [far_total, of_plane(0)] + [swap(of_plane(m), "hrow", m) for m in range(1, near)]
    )
    shock_of = pair_index[:, 0, None, None]
    output_of = pair_index[:, 1, None, None]
    picked = jnp.zeros((pairs, cols, rows), jnp.float32)
    for s in range(shocks):
        for o in range(outputs):
            one = total[s, :, o * rows : (o + 1) * rows]
            picked = jnp.where((shock_of == s) & (output_of == o), one, picked)
    return jnp.swapaxes(picked, 1, 2)


def solution(mesh):
    placed = (P(None, "hrow", "hcol"), P(None, "hrow", "hcol"), P(None, None, "hcol"), P())
    return jax.shard_map(
        shards, mesh=mesh, in_specs=placed, out_specs=P(None, "hrow", "hcol"), check_vma=False
    )
```
